32 devices in a mesh: dp: 16 (over z, x, core), expert: 2 (over y).
Axes of the slice: x: 2, y: 2, z: 4, core: 2. Of those that a mesh axis runs over, the one named last changes fastest.
Arguments:
- grad_out: bfloat16 [4096, 2560], P(('dp', 'expert')), may hold values from -6 to 6
- saved_input: bfloat16 [4096, 2560], P(('dp', 'expert')), may hold values from -6 to 6
- expert_ids: int32 [4096, 2], P(('dp', 'expert')), may hold values from 0 to 3, all different within a row; in each aligned block of 128 rows (0 to 127, 128 to 255, ...) at most 128 rows name the same one
- gate_weights: float32 [4096, 2], P(('dp', 'expert')), may hold values from 0.2 to 1
- up_weight: bfloat16 [4, 2560, 512], P('expert', 'dp'), may hold values from -0.125 to 0.125
- down_weight: bfloat16 [4, 512, 2560], P('expert', 'dp'), may hold values from -0.25 to 0.25
- engram_gate: float32 [4096, 4], P(('dp', 'expert')), may hold values from 0.1 to 1
- memory_owner: int32 [4096, 4], P(('dp', 'expert')), may hold values from 0 to 15, all different within a row; in each aligned block of 128 rows (0 to 127, 128 to 255, ...) at most 64 rows name the same one
- memory_slot: int32 [4096, 4], P(('dp', 'expert')), may hold values from 0 to 127
Outputs:
- grad_input: bfloat16 [4096, 2560], P(('dp', 'expert'))
- table_grad: float32 [4, 2048, 1280], P(None, ('dp', 'expert'))
The draws below stay inside these ranges and needn't reach their ends.
Inputs may be any that keep to these rules, and one draw needn't show every extreme that they name: `expert_ids`: each row names 2 different experts; among the rows of one device (aligned blocks of 128 rows) no expert is named more than 128 times, a bound that some block reaches. `memory_owner`: each row names 4 different owners; among the rows of one device (aligned blocks of 128 rows) no owner is named more than 64 times, a bound that some block reaches.
All inputs are finite; a program needn't handle non-finite values.
Results may differ from the reference program's by a relative error of at most 0.014.
Values may be sent and summed in bfloat16 or wider, within the bound.
No kernel may reach another device: no remote copies, remote signals or barrier semaphores. Data moves between devices by JAX's collectives and lax.ppermute only.
A program may use at most 128 MiB of HBM per device.

```python
import math
import jax
import jax.numpy as jnp
import numpy as np
from jax import lax

D = 2560
HID = 512
TOP = 2
HEADS = 2
TOK_DEV = 128
SHARD = 128
EXPERTS = 4
TOKENS = 4096
ECAP = 128
LOOKUPS = 4
CAP = 64
TABLE_ROWS = 2048
N_DP = 16
N_EXPERT = 2


def plant(entries, rng, smallest, top_value):
    dims = entries.shape
    index_at = [jax.random.randint(jax.random.fold_in(rng, axis), (), 0, dims[axis]) for axis in range(len(dims))]
    entries = entries.at[tuple(index_at)].set(smallest)
    longest = dims.index(max(dims))
    index_at[longest] = (index_at[longest] + 1) % dims[longest]
    return entries.at[tuple(index_at)].set(top_value)


def shard_levels(own_key, dims, split, least, high):
    level = 1.0
    for axis_at, shards_of in split:
        draws = jax.random.uniform(jax.random.fold_in(jax.random.fold_in(own_key, 6), axis_at), (shards_of,), jnp.float32, least / len(split), high / len(split))
        level = level * jnp.repeat(jnp.exp(draws), dims[axis_at] // shards_of).reshape((-1,) + (1,) * (len(dims) - 1 - axis_at))
    return level


def rank_table(amount, skew):
    loads = [(1 << 20) // math.isqrt(standing ** skew) + 1 for standing in range(1, amount + 1)]
    scale = 1 + sum(loads) // (1 << 30)
    return np.cumsum(np.array([max(1, weight // scale) for weight in loads]))


def skewed_ids(stream_key, extent, count, skew):
    grid = rank_table(count, skew)
    lot = jax.random.randint(jax.random.fold_in(stream_key, 1), extent, 0, int(grid[count - 1]))
    grade = jnp.searchsorted(jnp.asarray(grid, jnp.int32), lot, side="right")
    return jax.random.permutation(jax.random.fold_in(stream_key, 2), count)[grade].astype(jnp.int32)


def assign_block(rng, own, number, rows, number_of, top, reach, skew):
    order = jax.random.permutation(rng, number_of)
    crowded, common = load_shares(number_of, rows * top, reach, skew, True), load_shares(number_of, rows * top, reach, skew, False)
    places = jnp.arange(number_of)

    def named(tallies, rotation):
        used = int((tallies > 0).sum())
        fixed = max(1, used // 4)
        passed = fixed + (places - fixed + rotation * (used - fixed)) % max(1, number_of - fixed)
        return jnp.zeros((number_of,), jnp.int32).at[order[jnp.where(places < fixed, places, passed)]].set(jnp.asarray(tallies, jnp.int32))

    tallies = jnp.where(number % 4 == 0, named(crowded, number // 4), named(common, number - number // 4 - 1))
    mixed = jax.random.permutation(jax.random.fold_in(own, 3), number_of)
    giver, receiver = mixed[0:number_of // 2 * 2:2], mixed[1:number_of // 2 * 2:2]
    margin = jnp.minimum(tallies[giver] - 1, reach - tallies[receiver]) // 2
    margin = jnp.where((giver == order[0]) | (receiver == order[0]) | (tallies[receiver] == 0), 0, jnp.maximum(margin, 0))
    passed = jax.random.randint(jax.random.fold_in(own, 4), (number_of // 2,), 0, 1 << 20) % (margin + 1)
    tallies = tallies.at[giver].add(-passed).at[receiver].add(passed)
    labels = jnp.searchsorted(jnp.cumsum(tallies), jnp.arange(rows * top), side="right").astype(jnp.int32)
    grid = labels.reshape(top, rows).T
    grid = grid[jax.random.permutation(jax.random.fold_in(own, 1), rows)]
    rotation = jax.random.randint(jax.random.fold_in(own, 2), (rows, 1), 0, top)
    return jnp.take_along_axis(grid, (jnp.arange(top)[None, :] + rotation) % top, axis=1)


def load_shares(number_of, total, limit, skew, full):
    weights = [(1 << 20) // math.isqrt(grade ** skew) + 1 for grade in range(1, number_of + 1)]
    largest = limit if full else min(limit, max(-(-total // number_of), total * weights[0] // sum(weights)))
    least = 1 if total - largest >= number_of - 1 else 0
    given, surplus = [largest] + [least] * (number_of - 1), total - largest - least * (number_of - 1)
    while surplus > 0:
        candidates = [i for i in range(1, number_of) if given[i] < largest] or [i for i in range(1, number_of) if given[i] < limit]
        pool, budget = sum([weights[i] for i in candidates]), surplus
        for i in candidates:
            addition = min(limit - given[i], max(1, budget * weights[i] // pool), surplus)
            given[i] = given[i] + addition
            surplus = surplus - addition
    return np.array(given)


def scatter_about(stream_key, dims, deviation, limit, shards=(), kind=jnp.bfloat16):
    drawn = deviation * jax.random.normal(stream_key, dims, jnp.float32)
    if shards:
        drawn = drawn * shard_levels(stream_key, dims, shards, -0.22, 0.18)
    return jnp.clip(drawn, -limit, limit).astype(kind)


def setup_inputs(seed: int = 0) -> dict:
    key_of = jax.random.split(jax.random.key(seed), 10)
    grad_out = scatter_about(key_of[0], (TOKENS, D), 1.0, 6.0, ((0, 32),))
    saved_input = scatter_about(key_of[1], (TOKENS, D), 1.0, 6.0, ((0, 32),))
    expert_ids_keys = jax.random.split(jax.random.fold_in(key_of[2], 1), TOKENS // TOK_DEV)
    expert_ids_turns = jax.random.permutation(jax.random.fold_in(key_of[2], 3), TOKENS // TOK_DEV)
    expert_ids = jax.vmap(lambda own, number: assign_block(jax.random.fold_in(key_of[2], 2), own, number, TOK_DEV, EXPERTS, TOP, ECAP, 2))(expert_ids_keys, expert_ids_turns).reshape((TOKENS, TOP))
    gate_weights = jnp.clip(0.2 + 0.8 * jax.random.uniform(key_of[3], (TOKENS, TOP), jnp.float32) ** shard_levels(key_of[3], (TOKENS, TOP), ((0, 32),), -0.2, 0.2), 0.2, 1.0)
    up_weight = scatter_about(key_of[4], (EXPERTS, D, HID), D ** -0.5, 0.125, ((0, 2), (1, 16)))
    down_weight = scatter_about(key_of[5], (EXPERTS, HID, D), HID ** -0.5, 0.25, ((0, 2), (1, 16)))
    engram_gate = jnp.clip(0.1 + 0.9 * jax.random.uniform(key_of[6], (TOKENS, LOOKUPS), jnp.float32) ** shard_levels(key_of[6], (TOKENS, LOOKUPS), ((0, 32),), -0.2, 0.2), 0.1, 1.0)
    memory_owner_keys = jax.random.split(jax.random.fold_in(key_of[7], 1), TOKENS // TOK_DEV)
    memory_owner_turns = jax.random.permutation(jax.random.fold_in(key_of[7], 3), TOKENS // TOK_DEV)
    memory_owner = jax.vmap(lambda own, number: assign_block(jax.random.fold_in(key_of[7], 2), own, number, TOK_DEV, N_DP, LOOKUPS, CAP, 2))(memory_owner_keys, memory_owner_turns).reshape((TOKENS, LOOKUPS))
    memory_slot = plant(skewed_ids(key_of[8], (TOKENS, LOOKUPS), SHARD, 2), jax.random.fold_in(key_of[8], 3), 0, SHARD - 1).astype(jnp.int32)
    return {"grad_out": grad_out, "saved_input": saved_input, "expert_ids": expert_ids, "gate_weights": gate_weights, "up_weight": up_weight, "down_weight": down_weight, "engram_gate": engram_gate, "memory_owner": memory_owner, "memory_slot": memory_slot}


def silu_slope(pre):
    sig = jax.nn.sigmoid(pre)
    return sig * (1.0 + pre * (1.0 - sig))


def reference(grad_out, saved_input, expert_ids, gate_weights, up_weight, down_weight, engram_gate, memory_owner, memory_slot):
    tokens = grad_out.shape[0]
    most = N_DP * N_EXPERT * ECAP

    def per_expert(total, expert):
        hits = expert_ids == expert
        chosen = jnp.any(hits, axis=1)
        weight = jnp.sum(jnp.where(hits, gate_weights, jnp.zeros_like(gate_weights)), axis=1)
        index = jnp.nonzero(chosen, size=most, fill_value=0)[0].astype(jnp.int32)
        valid = jnp.arange(most, dtype=jnp.int32) < jnp.sum(chosen.astype(jnp.int32))
        inputs = saved_input[index]
        grads = grad_out[index]
        up_one = lax.dynamic_index_in_dim(up_weight, expert, 0, keepdims=False)
        down_one = lax.dynamic_index_in_dim(down_weight, expert, 0, keepdims=False)
        pre = jnp.dot(inputs, up_one, preferred_element_type=jnp.float32)
        back = jnp.dot(grads, down_one.T, preferred_element_type=jnp.float32)
        slope = (back * silu_slope(pre)).astype(jnp.bfloat16)
        expert_grad = jnp.dot(slope, up_one.T, preferred_element_type=jnp.float32).astype(jnp.bfloat16)
        term = jnp.where(valid[:, None], weight[index][:, None] * expert_grad.astype(jnp.float32), 0.0)
        return total.at[index].add(term), None

    total, unused = lax.scan(per_expert, jnp.zeros((tokens, D), jnp.float32), jnp.arange(EXPERTS, dtype=jnp.int32))
    width = D // 2
    halves = grad_out.reshape(tokens, 2, width)
    rows = (engram_gate[:, :, None] * jnp.repeat(halves, HEADS, axis=1).astype(jnp.float32)).astype(jnp.bfloat16)
    target = (jnp.arange(LOOKUPS, dtype=jnp.int32)[None, :] * TABLE_ROWS + memory_owner * SHARD + memory_slot).reshape(-1)
    table = jnp.zeros((LOOKUPS * TABLE_ROWS, width), jnp.float32).at[target].add(rows.reshape(-1, width).astype(jnp.float32))
    return total.astype(jnp.bfloat16), table.reshape(LOOKUPS, TABLE_ROWS, width)
```

```python
import functools

import jax
import jax.numpy as jnp
from jax import lax
from jax.experimental import pallas as pl
from jax.experimental.pallas import tpu as pltpu
from jax.sharding import PartitionSpec as P

ORDERS = 2
SHARD = 128
LANES = 128


def silu_slope(pre):
    sig = jax.nn.sigmoid(pre)
    return sig * (1.0 + pre * (1.0 - sig))


def swap(value, bit):
    size = lax.axis_size("dp")
    return lax.ppermute(value, "dp", [(i, i ^ bit) for i in range(size)])


def over_expert(value, step):
    size = lax.axis_size("expert")
    return lax.ppermute(value, "expert", [(i, (i + step) % size) for i in range(size)])


def over_even(value):
    size = lax.axis_size("dp")
    pairs = []
    for i in range(size):
        z = i // 4
        to = i if z in (0, size // 4 - 1) else (i + 4 if z % 2 else i - 4)
        pairs.append((i, to))
    return lax.ppermute(value, "dp", pairs)


def pick(by_plane, plane):
    value = by_plane[-1]
    for z in range(len(by_plane) - 2, -1, -1):
        if by_plane[z] is not by_plane[z + 1]:
            value = jnp.where(plane <= z, by_plane[z], value)
    return value


def arrivals(planes):
    orders = []
    for z in range(planes):
        order = []
        for step in range(1, planes):
            for kind in (0, 1):
                offset = step if (z + kind) % 2 == 0 else -step
                if 0 <= z + offset < planes:
                    order.append((step, kind, offset))
        orders.append(order)
    return orders


def prepare_kernel(up_ref, down_ref, grad_ref, *refs):
    ids_ref, weights_ref, gate_ref, owner_ref, slot_ref, packed_ref, rows_ref, meta_ref = refs
    blocks, rows, cols = packed_ref.shape[1] // 2, packed_ref.shape[2], packed_ref.shape[3]
    for e in range(packed_ref.shape[0]):
        for b in range(blocks):
            packed_ref[e, b] = up_ref[e, b * rows : (b + 1) * rows, :]
            packed_ref[e, blocks + b] = down_ref[e, :, b * cols : (b + 1) * cols]
    tok, width = grad_ref.shape
    rows_ref[:, pl.ds(0, width)] = grad_ref[...]
    weights = weights_ref[...]
    high = weights.astype(jnp.bfloat16).astype(jnp.float32)
    meta_ref[...] = jnp.zeros_like(meta_ref)
    at = 0
    for value in (
        owner_ref[...].astype(jnp.float32),
        slot_ref[...].astype(jnp.float32),
        gate_ref[...],
        ids_ref[...].astype(jnp.float32),
        high,
        weights - high,
    ):
        meta_ref[pl.ds(at, value.shape[0]), :] = value
        at += value.shape[0]
    rows_ref[:, pl.ds(width, LANES)] = meta_ref[...].T.astype(jnp.bfloat16)


def prepare(up, down, grad_out, expert_ids, gate_weights, engram_gate, owner, slot):
    experts, _, hid = up.shape
    rows, width = down.shape[1:]
    tok = grad_out.shape[0]
    return pl.pallas_call(
        prepare_kernel,
        out_shape=(
            jax.ShapeDtypeStruct((experts, 2 * (width // hid), rows, hid), up.dtype),
            jax.ShapeDtypeStruct((tok, width + LANES), grad_out.dtype),
        ),
        scratch_shapes=[pltpu.VMEM((LANES, tok), jnp.float32)],
    )(up, down, grad_out, expert_ids.T, gate_weights.T, engram_gate.T, owner.T, slot.T)


def table_kernel(lookups, planes, place_ref, *refs):
    blocks = refs[: -planes - 2]
    outs, tokens, sem = refs[-planes - 2 : -2], refs[-2], refs[-1]
    tok, total = blocks[0].shape
    width = total - LANES
    half = width // ORDERS
    heads = lookups // ORDERS
    part = outs[0].shape[0] // lookups
    copies = []
    for b, block in enumerate(blocks):
        copy = pltpu.make_async_copy(block, tokens.at[pl.ds(b * tok, tok)], sem.at[b])
        copy.start()
        copies.append(copy)
    for copy in copies:
        copy.wait()
    count = tok * len(blocks)
    metas = [
        tokens[pl.ds(b * tok, tok), pl.ds(width, LANES)].astype(jnp.float32).T
        for b in range(len(blocks))
    ]
    meta = jnp.concatenate([m[: 3 * lookups] for m in metas], axis=1)
    key = meta[:lookups] * SHARD + meta[lookups : 2 * lookups]
    gate = meta[2 * lookups :]
    me, expert = place_ref[0], place_ref[1]
    plane = me // 4
    row = lax.broadcasted_iota(jnp.int32, (part, count), 0)
    for o in range(ORDERS):
        hits = []
        for offset in range(planes):
            to = lax.rem(jnp.where(plane % 2 == 0, plane + offset, plane + planes - offset), planes)
            to = to * 4 + me % 4
            rows = (row + (to * SHARD + expert * part)).astype(jnp.float32)
            for j in range(o * heads, (o + 1) * heads):
                hit = jnp.where(rows == key[j : j + 1], gate[j : j + 1], 0.0)
                hits.append(hit.astype(jnp.bfloat16))
        sums = jnp.dot(
            jnp.concatenate(hits, axis=0),
            tokens[:, pl.ds(o * half, half)],
            preferred_element_type=jnp.float32,
        )
        size = heads * part
        for offset in range(planes):
            outs[offset][pl.ds(o * size, size), :] = sums[
                offset * size : (offset + 1) * size
            ].astype(outs[offset].dtype)


def table_sums(blocks, place, lookups, part):
    tok, total = blocks[0].shape
    half = (total - LANES) // ORDERS
    planes = lax.axis_size("dp") // 4
    rows = lookups * part
    return pl.pallas_call(
        functools.partial(table_kernel, lookups, planes),
        out_shape=tuple(
            jax.ShapeDtypeStruct((rows, half), jnp.bfloat16 if offset else jnp.float32)
            for offset in range(planes)
        ),
        in_specs=[pl.BlockSpec(memory_space=pltpu.SMEM)]
        + [pl.BlockSpec(memory_space=pl.ANY)] * len(blocks),
        scratch_shapes=[
            pltpu.VMEM((tok * len(blocks), total), jnp.bfloat16),
            pltpu.SemaphoreType.DMA((len(blocks),)),
        ],
        compiler_params=pltpu.CompilerParams(vmem_limit_bytes=56 << 20),
        cost_estimate=pl.CostEstimate(
            flops=2 * planes * rows * tok * len(blocks) * half,
            bytes_accessed=2 * tok * len(blocks) * total + 2 * planes * rows * half,
            transcendentals=0,
        ),
    )(place, *blocks)


def ffn_kernel(where, groups, planes, lookups, top, *refs):
    place_ref, tokens, refs = refs[0], refs[1 : 1 + 2 * groups], refs[1 + 2 * groups :]
    pieces, refs = refs[: len(where)], refs[len(where) :]
    own_ref, rest_ref, grad, inp, up, down, token_sem, piece_sem = refs
    tok, width = own_ref.shape
    experts, blocks, size, rows, hid = down.shape
    me, expert = place_ref[0], place_ref[1]
    plane = me // 4

    token_copies = []
    for g in range(groups):
        for source, target, sem in ((tokens[g], grad, 0), (tokens[groups + g], inp, 1)):
            copy = pltpu.make_async_copy(
                source, target.at[pl.ds(g * tok, tok)], token_sem.at[sem, g]
            )
            copy.start()
            token_copies.append(copy)
    ups, downs = [], []
    for number, (offsets, flip) in enumerate(where):
        at = jnp.bitwise_xor(me, flip)
        for z, offset in enumerate(offsets):
            if offset:
                at = at + jnp.where(plane == z, 4 * offset, 0)
        copy = pltpu.make_async_copy(
            pieces[number].at[:, pl.ds(0, blocks)],
            up.at[:, pl.ds(at * blocks, blocks)],
            piece_sem.at[0, number],
        )
        copy.start()
        ups.append(copy)
        copy = pltpu.make_async_copy(
            pieces[number].at[:, pl.ds(blocks, blocks)],
            down.at[:, :, at],
            piece_sem.at[1, number],
        )
        copy.start()
        downs.append(copy)
    for copy in token_copies + ups + downs:
        copy.wait()

    def up_block(e, b):
        return up[e, b * size : (b + 1) * size].reshape(size * rows, hid)

    chunk = 2 * tok if groups % 2 == 0 else tok
    for start in range(0, groups * tok, chunk):
        span = pl.ds(start, chunk)
        meta = grad[span, pl.ds(width, LANES)].astype(jnp.float32)
        at = 3 * lookups
        slopes = []
        for e in range(experts):
            pre = jnp.zeros((chunk, hid), jnp.float32)
            back = jnp.zeros((chunk, hid), jnp.float32)
            for b in range(blocks):
                cols = pl.ds(b * hid, hid)
                pre += jnp.dot(inp[span, cols], up_block(e, b), preferred_element_type=jnp.float32)
                back += lax.dot_general(
                    grad[span, cols],
                    down[e, b].reshape(size * rows, hid),
                    (((1,), (1,)), ((), ())),
                    preferred_element_type=jnp.float32,
                )
            weight = jnp.zeros((chunk, 1), jnp.float32)
            number = (expert * experts + e).astype(jnp.float32)
            for k in range(top):
                value = meta[:, at + top + k : at + top + k + 1]
                value += meta[:, at + 2 * top + k : at + 2 * top + k + 1]
                weight += jnp.where(meta[:, at + k : at + k + 1] == number, value, 0.0)
            slopes.append((back * silu_slope(pre) * weight).astype(jnp.bfloat16))
        for b in range(blocks):
            cols = pl.ds(b * hid, hid)
            total = jnp.zeros((chunk, hid), jnp.float32)
            for e in range(experts):
                total += lax.dot_general(
                    slopes[e],
                    up_block(e, b),
                    (((1,), (1,)), ((), ())),
                    preferred_element_type=jnp.float32,
                )
            if start == 0:
                own_ref[:, cols] = total[:tok]
                if chunk > tok:
                    rest_ref[pl.ds(0, chunk - tok), cols] = total[tok:].astype(jnp.bfloat16)
            else:
                rest_ref[pl.ds(start - tok, chunk), cols] = total.astype(jnp.bfloat16)


def expert_layers(grads, inputs, pieces, place, lookups, top):
    groups = len(grads)
    tok, width = inputs[0].shape
    experts, blocks2, rows, hid = pieces[0][0].shape
    blocks = blocks2 // 2
    dp = lax.axis_size("dp")
    where = tuple((tuple(offsets), flip) for _, offsets, flip in pieces)
    rest_rows = max(groups - 1, 1) * tok
    return pl.pallas_call(
        functools.partial(ffn_kernel, where, groups, dp // 4, lookups, top),
        out_shape=(
            jax.ShapeDtypeStruct((tok, width), jnp.float32),
            jax.ShapeDtypeStruct((rest_rows, width), jnp.bfloat16),
        ),
        in_specs=[pl.BlockSpec(memory_space=pltpu.SMEM)]
        + [pl.BlockSpec(memory_space=pl.ANY)] * (2 * groups + len(pieces)),
        out_specs=(
            pl.BlockSpec(memory_space=pltpu.VMEM),
            pl.BlockSpec(memory_space=pltpu.VMEM),
        ),
        scratch_shapes=[
            pltpu.VMEM((groups * tok, width + LANES), jnp.bfloat16),
            pltpu.VMEM((groups * tok, width), jnp.bfloat16),
            pltpu.VMEM((experts, dp * blocks, rows, hid), jnp.bfloat16),
            pltpu.VMEM((experts, blocks, dp, rows, hid), jnp.bfloat16),
            pltpu.SemaphoreType.DMA((2, groups)),
            pltpu.SemaphoreType.DMA((2, len(pieces))),
        ],
        compiler_params=pltpu.CompilerParams(vmem_limit_bytes=56 << 20),
        cost_estimate=pl.CostEstimate(
            flops=6 * groups * tok * width * hid * experts,
            bytes_accessed=4 * experts * width * hid + 12 * groups * tok * width,
            transcendentals=groups * tok * hid * experts,
        ),
    )(place, *grads, *inputs, *[piece[0] for piece in pieces])


def per_device(
    grad_out,
    saved_input,
    expert_ids,
    gate_weights,
    up_weight,
    down_weight,
    engram_gate,
    memory_owner,
    memory_slot,
):
    tok, width = grad_out.shape
    lookups, top = engram_gate.shape[1], expert_ids.shape[1]
    groups = lax.axis_size("expert")
    planes = lax.axis_size("dp") // 4
    part = SHARD // groups
    me = lax.axis_index("dp")
    plane = me // 4
    place = jnp.stack([me, lax.axis_index("expert")]).astype(jnp.int32)
    others = range(1, groups)
    fence = lax.optimization_barrier

    packed, rows = prepare(
        up_weight,
        down_weight,
        grad_out,
        expert_ids,
        gate_weights,
        engram_gate,
        memory_owner,
        memory_slot,
    )
    orders = arrivals(planes)
    came = {}
    zero = (0,) * planes
    pieces = [(packed, zero, 0)]
    blocks = [rows]
    grads = [rows]

    def along(step, line):
        even = over_even(line[0]) if step < planes - 1 else None
        return swap(line[1], 4), even

    def arrival(number):
        by_plane = [came[order[number][0]][order[number][1]] for order in orders]
        return pick(by_plane, plane), tuple(order[number][2] for order in orders)

    inner = jnp.logical_and(plane > 0, plane < planes - 1)

    def plus(share, came_in, even):
        came_in = came_in.astype(jnp.float32)
        if even:
            came_in = jnp.where(inner, came_in, 0.0)
        return share.astype(jnp.float32) + came_in

    def reduce(step, sums):
        odd, even = partials[planes - step], partials[step]
        if step > 1 and sums[1] is not None:
            odd = plus(odd, sums[1], True).astype(jnp.bfloat16)
        even = over_even(plus(even, sums[0], False).astype(jnp.bfloat16)) if step > 1 else None
        return swap(odd, 4), even

    def together(near, line, over_y, over_x, *rest):
        near, line, over_y, over_x, rest = fence((near, line[::-1], over_y, over_x, rest))
        return near, line[::-1], over_y, over_x, rest

    near = swap(rows, 1)
    line = along(1, (packed, packed))
    got = [over_expert(rows, step) for step in others]
    rows_x = swap(rows, 2)
    near, line, got, rows_x, (late,) = together(near, line, got, rows_x, packed)
    came[1] = line
    grads += got
    blocks += [near, rows_x] + got

    near = swap(rows_x, 1)
    line = along(2, line) if planes > 2 else line
    far = [over_expert(rows_x, step) for step in others]
    own_x = swap(late, 2)
    value, where = arrival(0)
    near, line, far, passed, (value, later) = together(near, line, far, own_x, value, saved_input)
    came[min(2, planes - 1)] = line
    blocks += [near] + far
    pieces += [(passed, zero, 2)]
    waiting = [(packed, zero, 1), (passed, zero, 3)]

    sums, inputs = (), []
    for number in range(1, planes):
        pieces += [(value, where, 0)]
        moved, waiting = waiting, [(value, where, 1)]
        next_value = next_at = ()
        if number + 1 < planes:
            next_value, next_at = arrival(number)
        if number == 1:
            near = [swap(block, 1) for block in got + far]
            partials = table_sums(blocks + near, place, lookups, part)
            moved, waiting = [], moved + waiting
            inputs = [over_expert(later, step) for step in others]
        elif number + 1 == planes:
            moved, waiting = moved[:2], moved[2:] + waiting
        near = [swap(entry[0], 1) for entry in moved]
        if number + 2 < planes:
            line = along(number + 2, line)
        if number > 1:
            sums = reduce(number - 1, sums)
        near, line, (inputs, sums), passed, (partials, value) = together(
            near, line, (inputs, sums[::-1]), swap(value, 2), partials, next_value
        )
        sums = sums[::-1]
        pieces += [(core, at, flip) for core, (_, at, flip) in zip(near, moved)]
        pieces += [(passed, where, 2)]
        waiting += [(passed, where, 3)]
        came[min(number + 2, planes - 1)] = line
        where = next_at
    inputs = [saved_input] + inputs

    sums = reduce(planes - 1, sums)
    pieces += [(swap(value, 1), at, flip) for value, at, flip in waiting]
    total, rest = expert_layers(grads, inputs, pieces, place, lookups, top)
    total, sums = fence((total, sums))
    for back in others:
        value = rest[(back - 1) * tok : back * tok]
        total = total + over_expert(value, groups - back).astype(jnp.float32)
    table = partials[0]
    for came_in, even in zip(sums, (False, True)):
        if came_in is not None:
            table = plus(table, came_in, even)
    return total.astype(jnp.bfloat16), table.reshape(lookups, part, width // ORDERS)


def solution(mesh):
    return jax.shard_map(
        per_device,
        mesh=mesh,
        in_specs=(
            P(("dp", "expert"), None),
            P(("dp", "expert"), None),
            P(("dp", "expert"), None),
            P(("dp", "expert"), None),
            P("expert", "dp", None),
            P("expert", "dp", None),
            P(("dp", "expert"), None),
            P(("dp", "expert"), None),
            P(("dp", "expert"), None),
        ),
        out_specs=(P(("dp", "expert"), None), P(None, ("dp", "expert"), None)),
        check_vma=False,
    )
```

```python
import functools
import math

import jax
import jax.numpy as jnp
from jax import lax
from jax.experimental import pallas as pl
from jax.experimental.pallas import tpu as pltpu
from jax.sharding import PartitionSpec as P

ORDERS = 2
SHARD = 128
LANES = 128


def silu_slope(pre):
    sig = jax.nn.sigmoid(pre)
    return sig * (1.0 + pre * (1.0 - sig))


def swap(value, bit):
    size = lax.axis_size("dp")
    return lax.ppermute(value, "dp", [(i, i ^ bit) for i in range(size)])


def over_expert(value, step):
    size = lax.axis_size("expert")
    return lax.ppermute(value, "expert", [(i, (i + step) % size) for i in range(size)])


def over_even(value):
    planes = lax.axis_size("dp") // 4
    pairs = []
    for z in range(1, planes - 1, 2):
        for i in range(z * 4, z * 4 + 4):
            pairs += [(i, i + 4), (i + 4, i)]
    return lax.ppermute(value, "dp", pairs)


def pick(by_plane, plane):
    value = by_plane[-1]
    for z in range(len(by_plane) - 2, -1, -1):
        if by_plane[z] is not by_plane[z + 1]:
            value = jnp.where(plane <= z, by_plane[z], value)
    return value


def arrivals(planes):
    orders = []
    for z in range(planes):
        order = []
        for step in range(1, planes):
            for kind in (0, 1):
                offset = step if (z + kind) % 2 == 0 else -step
                if 0 <= z + offset < planes:
                    order.append((step, kind, offset))
        orders.append(order)
    return orders


def prepare_kernel(up_ref, down_ref, grad_ref, *refs):
    ids_ref, weights_ref, gate_ref, owner_ref, slot_ref, packed_ref, rows_ref, meta_ref = refs
    blocks, rows, cols = packed_ref.shape[1] // 2, packed_ref.shape[2], packed_ref.shape[3]
    for e in range(packed_ref.shape[0]):
        for b in range(blocks):
            packed_ref[e, b] = up_ref[e, b * rows : (b + 1) * rows, :]
            packed_ref[e, blocks + b] = down_ref[e, :, b * cols : (b + 1) * cols]
    tok, width = grad_ref.shape
    rows_ref[:, pl.ds(0, width)] = grad_ref[...]
    weights = weights_ref[...]
    high = weights.astype(jnp.bfloat16).astype(jnp.float32)
    meta_ref[...] = jnp.zeros_like(meta_ref)
    at = 0
    for value in (
        owner_ref[...].astype(jnp.float32),
        slot_ref[...].astype(jnp.float32),
        gate_ref[...],
        ids_ref[...].astype(jnp.float32),
        high,
        weights - high,
    ):
        meta_ref[pl.ds(at, value.shape[0]), :] = value
        at += value.shape[0]
    rows_ref[:, pl.ds(width, LANES)] = meta_ref[...].T.astype(jnp.bfloat16)


def prepare(up, down, grad_out, expert_ids, gate_weights, engram_gate, owner, slot):
    experts, _, hid = up.shape
    rows, width = down.shape[1:]
    tok = grad_out.shape[0]
    return pl.pallas_call(
        prepare_kernel,
        out_shape=(
            jax.ShapeDtypeStruct((experts, 2 * (width // hid), rows, hid), up.dtype),
            jax.ShapeDtypeStruct((tok, width + LANES), grad_out.dtype),
        ),
        scratch_shapes=[pltpu.VMEM((LANES, tok), jnp.float32)],
    )(up, down, grad_out, expert_ids.T, gate_weights.T, engram_gate.T, owner.T, slot.T)


def unstacked(refs):
    dims = min(ref.ndim for ref in refs)
    blocks = []
    for ref in refs:
        blocks += [ref] if ref.ndim == dims else [ref.at[i] for i in range(ref.shape[0])]
    return blocks


def folded(rows, width, shape):
    _, count, deep, wide = shape
    return (
        shape[0] == ORDERS
        and width % (wide // 2) == 0
        and rows % (2 * deep) == 0
        and (width // (wide // 2)) * (rows // (2 * deep)) == count
    )


def folds(rows, width, shape):
    _, _, deep, wide = shape
    for b in range(width // (wide // 2)):
        for h in range(rows // (2 * deep)):
            for u in range(2):
                yield (
                    b * (rows // (2 * deep)) + h,
                    u * (wide // 2),
                    (2 * h + u) * deep,
                    b * (wide // 2),
                )


def table_kernel(lookups, part, planes, offsets, place_ref, *refs):
    count = len(offsets)
    blocks = unstacked(refs[: -count - 2])
    outs, tokens, sem = refs[-count - 2 : -2], refs[-2], refs[-1]
    width = tokens.shape[1] - LANES
    half = width // ORDERS
    heads = lookups // ORDERS
    copies, at = [], 0
    for b, block in enumerate(blocks):
        copies.append(
            pltpu.make_async_copy(block, tokens.at[pl.ds(at, block.shape[0])], sem.at[b])
        )
        at += block.shape[0]
    for copy in copies:
        copy.start()
    for copy in copies:
        copy.wait()
    metas = [
        tokens[pl.ds(first, LANES), pl.ds(width, LANES)].astype(jnp.float32).T
        for first in range(0, at, LANES)
    ]
    meta = jnp.concatenate([m[: 3 * lookups] for m in metas], axis=1)
    key = meta[:lookups] * SHARD + meta[lookups : 2 * lookups]
    gate = meta[2 * lookups :]
    me, expert = place_ref[0], place_ref[1]
    plane = me // 4
    row = lax.broadcasted_iota(jnp.int32, (part, at), 0)
    size = heads * part
    for o in range(ORDERS):
        hits = []
        for offset in offsets:
            to = lax.rem(jnp.where(plane % 2 == 0, plane + offset, plane + planes - offset), planes)
            to = to * 4 + me % 4
            rows = (row + (to * SHARD + expert * part)).astype(jnp.float32)
            for j in range(o * heads, (o + 1) * heads):
                hit = jnp.where(rows == key[j : j + 1], gate[j : j + 1], 0.0)
                hits.append(hit.astype(jnp.bfloat16))
        sums = jnp.dot(
            jnp.concatenate(hits, axis=0),
            tokens[:, pl.ds(o * half, half)],
            preferred_element_type=jnp.float32,
        )
        for number, out in enumerate(outs):
            value = sums[number * size : (number + 1) * size].astype(out.dtype)
            if len(out.shape) == 2:
                out[pl.ds(o * size, size), :] = value
                continue
            deep, wide = out.shape[2], out.shape[3] // 2
            for block, lane, at, column in folds(size, half, out.shape):
                out[o, block, :, pl.ds(lane, wide)] = value[at : at + deep, column : column + wide]


def table_sums(blocks, place, lookups, part, offsets, shape):
    total = blocks[0].shape[1]
    planes = lax.axis_size("dp") // 4
    rows, half = lookups * part, (total - LANES) // ORDERS
    count = sum(block.shape[0] for block in blocks)
    return pl.pallas_call(
        functools.partial(table_kernel, lookups, part, planes, tuple(offsets)),
        out_shape=tuple(
            jax.ShapeDtypeStruct(shape, jnp.bfloat16 if offset else jnp.float32)
            for offset in offsets
        ),
        in_specs=[pl.BlockSpec(memory_space=pltpu.SMEM)]
        + [pl.BlockSpec(memory_space=pl.ANY)] * len(blocks),
        scratch_shapes=[
            pltpu.VMEM((count, total), jnp.bfloat16),
            pltpu.SemaphoreType.DMA((len(blocks),)),
        ],
        compiler_params=pltpu.CompilerParams(vmem_limit_bytes=56 << 20),
        cost_estimate=pl.CostEstimate(
            flops=2 * len(offsets) * rows * count * half,
            bytes_accessed=2 * count * total + 2 * len(offsets) * rows * half,
            transcendentals=0,
        ),
    )(place, *blocks)


def table_total_kernel(*refs):
    values, out = refs[:-1], refs[-1]
    if len(values[0].shape) == 2:
        out[...] = sum(value[...].astype(jnp.float32) for value in values)
        return
    size, width = out.shape[0] // ORDERS, out.shape[1]
    deep, wide = values[0].shape[2], values[0].shape[3] // 2
    for o in range(ORDERS):
        for block, lane, at, column in folds(size, width, values[0].shape):
            out[pl.ds(o * size + at, deep), pl.ds(column, wide)] = sum(
                value[o, block, :, pl.ds(lane, wide)].astype(jnp.float32) for value in values
            )


def table_total(values, rows, width):
    return pl.pallas_call(
        table_total_kernel,
        out_shape=jax.ShapeDtypeStruct((rows, width), jnp.float32),
        compiler_params=pltpu.CompilerParams(vmem_limit_bytes=32 << 20),
    )(*values)


def located(where, place_ref, planes):
    offsets, flip = where
    me = place_ref[0]
    at = jnp.bitwise_xor(me, flip)
    for z, offset in enumerate(offsets):
        if offset:
            at = at + jnp.where(me // 4 == z, 4 * offset, 0)
    return at


def token_copies(tokens, targets, sem):
    groups = len(tokens) // 2
    tok = tokens[0].shape[0]
    copies = []
    for number, token in enumerate(tokens):
        target, g = targets[number // groups], number % groups
        copies.append(
            pltpu.make_async_copy(
                token, target.at[pl.ds(g * tok, tok)], sem.at[number // groups, g]
            )
        )
    return copies


def row_chunk(groups, tok):
    return 2 * tok if groups % 2 == 0 else tok


def hidden_kernel(where, last, groups, planes, *refs):
    place_ref, tokens, refs = refs[0], refs[1 : 1 + 2 * groups], refs[1 + 2 * groups :]
    pieces, refs = unstacked(refs[:-9]), refs[-9:]
    turned_ref, pre_ref, back_ref, grad, inp, up, down, token_sem, piece_sem = refs
    experts, blocks, size, rows, hid = down.shape
    copies = token_copies(tokens, (grad, inp), token_sem)
    for number, piece in enumerate(pieces):
        at = located(where[number], place_ref, planes)
        copies.append(
            pltpu.make_async_copy(
                piece.at[:, pl.ds(0, blocks)],
                up.at[:, pl.ds(at * blocks, blocks)],
                piece_sem.at[0, number],
            )
        )
        copies.append(
            pltpu.make_async_copy(
                piece.at[:, pl.ds(blocks, blocks)], down.at[:, :, at], piece_sem.at[1, number]
            )
        )
    for copy in copies:
        copy.start()
    for copy in copies:
        copy.wait()
    pair = located(last, place_ref, planes) // 2
    up[:, pl.ds(pair * 2 * blocks, 2 * blocks)] = jnp.zeros(
        (experts, 2 * blocks, rows, hid), up.dtype
    )
    tok = tokens[0].shape[0]
    chunk = row_chunk(groups, tok)
    for e in range(experts):
        for b in range(blocks):
            block = up[e, b * size : (b + 1) * size].reshape(size * rows, hid)
            turned_ref[e, :, pl.ds(b * hid, hid)] = block.T
    for start in range(0, groups * tok, chunk):
        span = pl.ds(start, chunk)
        for e in range(experts):
            pre = jnp.zeros((chunk, hid), jnp.float32)
            back = jnp.zeros((chunk, hid), jnp.float32)
            for b in range(blocks):
                cols = pl.ds(b * hid, hid)
                pre += jnp.dot(
                    inp[span, cols],
                    up[e, b * size : (b + 1) * size].reshape(size * rows, hid),
                    preferred_element_type=jnp.float32,
                )
                back += lax.dot_general(
                    grad[span, cols],
                    down[e, b].reshape(size * rows, hid),
                    (((1,), (1,)), ((), ())),
                    preferred_element_type=jnp.float32,
                )
            pre_ref[span, pl.ds(e * hid, hid)] = pre
            back_ref[span, pl.ds(e * hid, hid)] = back


def slab_of(blocks, rows):
    held = 2 * blocks * rows
    return held, -(-(LANES - math.gcd(held, LANES) + held) // LANES) * LANES


def result_kernel(last, groups, planes, lookups, top, *refs):
    place_ref, tokens, refs = refs[0], refs[1 : 1 + 2 * groups], refs[1 + 2 * groups :]
    turned_ref, first_ref, second_ref, pre_ref, back_ref, own_ref, rest_ref, *refs = refs
    grad, part, up, down, turned, pre_part, back_part, token_sem, piece_sem, turned_sem = refs
    tok, width = own_ref.shape
    experts, blocks, per, rows, hid = down.shape
    expert = place_ref[1]
    pair = located(last, place_ref, planes) // 2
    held, slab = slab_of(blocks, rows)
    base = pl.multiple_of(pair * held // LANES * LANES, LANES)
    skip = lax.rem(pair * held, LANES)

    up[...] = jnp.zeros_like(up)
    copies = token_copies(
        list(tokens[:groups]) + [token.at[:, pl.ds(base, slab)] for token in tokens[groups:]],
        (grad, part),
        token_sem,
    )
    for number, piece in enumerate((first_ref, second_ref)):
        at = located((last[0], last[1] + number), place_ref, planes)
        copies.append(
            pltpu.make_async_copy(
                piece.at[:, pl.ds(0, blocks)],
                up.at[:, pl.ds(skip // rows + lax.rem(at, 2) * blocks, blocks)],
                piece_sem.at[0, number],
            )
        )
        copies.append(
            pltpu.make_async_copy(
                piece.at[:, pl.ds(blocks, blocks)],
                down.at[:, :, lax.rem(at, per)],
                piece_sem.at[1, number],
            )
        )
    copies.append(pltpu.make_async_copy(pre_ref, pre_part, piece_sem.at[0, 2]))
    copies.append(pltpu.make_async_copy(back_ref, back_part, piece_sem.at[1, 2]))
    turns = [
        pltpu.make_async_copy(
            turned_ref.at[:, :, pl.ds(b * hid, hid)],
            turned.at[:, :, pl.ds(b * hid, hid)],
            turned_sem.at[b],
        )
        for b in range(blocks)
    ]
    for copy in copies + turns:
        copy.start()
    for copy in copies:
        copy.wait()

    hid_slab = pl.multiple_of(pair * 2 // per * LANES, LANES)
    hid_skip = lax.rem(pair * 2, per) * rows
    chunk = row_chunk(groups, tok)
    at = 3 * lookups
    lane = lax.broadcasted_iota(jnp.int32, (chunk, slab), 1)
    lane = jnp.logical_and(lane >= skip, lane < skip + held)
    hid_lane = lax.broadcasted_iota(jnp.int32, (chunk, LANES), 1)
    hid_lane = jnp.logical_and(hid_lane >= hid_skip, hid_lane < hid_skip + 2 * rows)
    for start in range(0, groups * tok, chunk):
        span = pl.ds(start, chunk)
        meta = grad[span, pl.ds(width, LANES)].astype(jnp.float32)
        mine = jnp.where(lane, part[span, :].astype(jnp.float32), 0.0).astype(jnp.bfloat16)
        slopes = []
        for e in range(experts):
            units = pl.ds(e * hid, hid)
            pre = pre_part[span, units] + jnp.dot(
                mine, up[e].reshape(slab, hid), preferred_element_type=jnp.float32
            )
            late = jnp.zeros((chunk, LANES), jnp.float32)
            for b in range(blocks):
                late += lax.dot_general(
                    grad[span, pl.ds(b * hid, hid)],
                    down[e, b].reshape(LANES, hid),
                    (((1,), (1,)), ((), ())),
                    preferred_element_type=jnp.float32,
                )
            lanes = pl.ds(pl.multiple_of(e * hid + hid_slab, LANES), LANES)
            back_part[span, lanes] = jnp.where(hid_lane, late, back_part[span, lanes])
            weight = jnp.zeros((chunk, 1), jnp.float32)
            number = (expert * experts + e).astype(jnp.float32)
            for k in range(top):
                value = meta[:, at + top + k : at + top + k + 1]
                value += meta[:, at + 2 * top + k : at + 2 * top + k + 1]
                weight += jnp.where(meta[:, at + k : at + k + 1] == number, value, 0.0)
            slope = back_part[span, units] * silu_slope(pre) * weight
            slopes.append(slope.astype(jnp.bfloat16))
        for b in range(blocks):
            cols = pl.ds(b * hid, hid)
            if start == 0:
                turns[b].wait()
            total = jnp.zeros((chunk, hid), jnp.float32)
            for e in range(experts):
                total += jnp.dot(
                    slopes[e], turned[e, :, cols], preferred_element_type=jnp.float32
                )
            if start == 0:
                own_ref[:, cols] = total[:tok]
                if chunk > tok:
                    rest_ref[pl.ds(0, chunk - tok), cols] = total[tok:].astype(jnp.bfloat16)
            else:
                rest_ref[pl.ds(start - tok, chunk), cols] = total.astype(jnp.bfloat16)
        late = jnp.zeros((chunk, slab), jnp.float32)
        for e in range(experts):
            late += lax.dot_general(
                slopes[e],
                up[e].reshape(slab, hid),
                (((1,), (1,)), ((), ())),
                preferred_element_type=jnp.float32,
            )
        cols = pl.ds(base, slab)
        if start == 0:
            own_ref[:, cols] += late[:tok]
            late, span = late[tok:], pl.ds(0, chunk - tok)
        else:
            span = pl.ds(start - tok, chunk)
        if start or chunk > tok:
            known = rest_ref[span, cols].astype(jnp.float32)
            rest_ref[span, cols] = (known + late).astype(jnp.bfloat16)


def hidden_layers(grads, inputs, pieces, last, place):
    groups = len(grads)
    tok, width = inputs[0].shape
    experts, blocks2, rows, hid = pieces[0][0].shape[-4:]
    blocks = blocks2 // 2
    dp = lax.axis_size("dp")
    where = tuple(entry for _, entries in pieces for entry in entries)
    any_space, vmem = pl.BlockSpec(memory_space=pl.ANY), pl.BlockSpec(memory_space=pltpu.VMEM)
    return pl.pallas_call(
        functools.partial(hidden_kernel, where, last, groups, dp // 4),
        out_shape=(
            jax.ShapeDtypeStruct((experts, hid, width), jnp.bfloat16),
            jax.ShapeDtypeStruct((groups * tok, experts * hid), jnp.float32),
            jax.ShapeDtypeStruct((groups * tok, experts * hid), jnp.float32),
        ),
        in_specs=[pl.BlockSpec(memory_space=pltpu.SMEM)]
        + [any_space] * (2 * groups + len(pieces)),
        out_specs=(vmem, vmem, vmem),
        scratch_shapes=[
            pltpu.VMEM((groups * tok, width + LANES), jnp.bfloat16),
            pltpu.VMEM((groups * tok, width), jnp.bfloat16),
            pltpu.VMEM((experts, dp * blocks, rows, hid), jnp.bfloat16),
            pltpu.VMEM((experts, blocks, dp, rows, hid), jnp.bfloat16),
            pltpu.SemaphoreType.DMA((2, groups)),
            pltpu.SemaphoreType.DMA((2, len(where))),
        ],
        compiler_params=pltpu.CompilerParams(vmem_limit_bytes=56 << 20),
        cost_estimate=pl.CostEstimate(
            flops=4 * groups * tok * width * hid * experts,
            bytes_accessed=6 * experts * width * hid + 8 * groups * tok * width,
            transcendentals=0,
        ),
    )(place, *grads, *inputs, *[piece[0] for piece in pieces])


def expert_results(grads, inputs, hidden, first, second, last, place, lookups, top):
    groups = len(grads)
    tok, width = inputs[0].shape
    experts, blocks2, rows, hid = first.shape
    blocks = blocks2 // 2
    dp = lax.axis_size("dp")
    turned, pre, back = hidden
    rest_rows = max(groups - 1, 1) * tok
    slab = slab_of(blocks, rows)[1]
    any_space, vmem = pl.BlockSpec(memory_space=pl.ANY), pl.BlockSpec(memory_space=pltpu.VMEM)
    return pl.pallas_call(
        functools.partial(result_kernel, last, groups, dp // 4, lookups, top),
        out_shape=(
            jax.ShapeDtypeStruct((tok, width), jnp.float32),
            jax.ShapeDtypeStruct((rest_rows, width), jnp.bfloat16),
        ),
        in_specs=[pl.BlockSpec(memory_space=pltpu.SMEM)] + [any_space] * (2 * groups + 5),
        out_specs=(vmem, vmem),
        scratch_shapes=[
            pltpu.VMEM((groups * tok, width + LANES), jnp.bfloat16),
            pltpu.VMEM((groups * tok, slab), jnp.bfloat16),
            pltpu.VMEM((experts, slab // rows, rows, hid), jnp.bfloat16),
            pltpu.VMEM((experts, blocks, LANES // rows, rows, hid), jnp.bfloat16),
            pltpu.VMEM(turned.shape, jnp.bfloat16),
            pltpu.VMEM(pre.shape, jnp.float32),
            pltpu.VMEM(back.shape, jnp.float32),
            pltpu.SemaphoreType.DMA((2, groups)),
            pltpu.SemaphoreType.DMA((2, 3)),
            pltpu.SemaphoreType.DMA((blocks,)),
        ],
        compiler_params=pltpu.CompilerParams(vmem_limit_bytes=60 << 20),
        cost_estimate=pl.CostEstimate(
            flops=2 * groups * tok * width * hid * experts,
            bytes_accessed=2 * experts * width * hid + 12 * groups * tok * width,
            transcendentals=groups * tok * hid * experts,
        ),
    )(place, *grads, *inputs, turned, first, second, pre, back)


def per_device(
    grad_out,
    saved_input,
    expert_ids,
    gate_weights,
    up_weight,
    down_weight,
    engram_gate,
    memory_owner,
    memory_slot,
):
    tok, width = grad_out.shape
    lookups, top = engram_gate.shape[1], expert_ids.shape[1]
    groups = lax.axis_size("expert")
    planes = lax.axis_size("dp") // 4
    part = SHARD // groups
    me = lax.axis_index("dp")
    plane = me // 4
    place = jnp.stack([me, lax.axis_index("expert")]).astype(jnp.int32)
    others = range(1, groups)
    fence = lax.optimization_barrier

    packed, rows = prepare(
        up_weight,
        down_weight,
        grad_out,
        expert_ids,
        gate_weights,
        engram_gate,
        memory_owner,
        memory_slot,
    )
    orders = arrivals(planes)
    came = {}
    zero = (0,) * planes

    def along(step, line):
        even = over_even(line[0]) if step < planes - 1 else None
        return swap(line[1], 4), even

    def arrival(number):
        by_plane = [came[order[number][0]][order[number][1]] for order in orders]
        offsets = tuple(order[number][2] for order in orders)
        return pick(by_plane, plane), offsets

    def plus(share, came_in):
        return (share.astype(jnp.float32) + came_in.astype(jnp.float32)).astype(jnp.bfloat16)

    def reduce(step, sums):
        odd, even = partials[planes - step], partials[step]
        if step > 1 and sums[1] is not None:
            odd = plus(odd, sums[1])
        even = over_even(plus(even, sums[0])) if step > 1 else None
        return swap(odd, 4), even

    half = width // ORDERS
    fits = planes > 3 and folded(lookups // ORDERS * part, half, packed.shape)
    shape = packed.shape if fits else (lookups * part, half)


    rows_x = swap(rows, 2)
    got = [over_expert(rows, step) for step in others]
    came[1] = along(1, (packed, packed))
    late, rows_x = fence((packed, rows_x))
    rows_x, got, near = fence((rows_x, got, swap(rows, 1)))
    grads = [rows] + got
    far = [over_expert(rows_x, step) for step in others]
    near = [near, swap(rows_x, 1)]
    if planes > 2:
        came[2] = along(2, came[1])
        got, far, near, came[2] = fence((got, far, near, came[2]))
    blocks = [rows, rows_x, *near, *got, *far]
    for block in got + far:
        blocks += [swap(block[: tok // 2], 1), swap(block[tok // 2 :], 1)]
    partials = table_sums(blocks, place, lookups, part, range(planes), shape)
    for step in range(3, planes - 1 if fits else planes):
        came[step] = along(step, came[step - 1])
    if fits:
        ends = jnp.logical_or(plane == 0, plane == planes - 1)
        met = swap(jnp.where(ends, partials[planes - 1], came[planes - 2][1]), 4)
        came[planes - 1] = (met, None)

    value, where = arrival(0)
    pair = jnp.stack([late, value])
    pair_x = swap(pair, 2)
    later, far = fence((saved_input, far))
    inputs = [over_expert(later, step) for step in others]

    pieces = [(pair, ((zero, 0), (where, 0)))]
    passed, passed_at = pair_x, ((zero, 2), (where, 2))
    todo, near, near_at = pieces[:1], [], []
    sums = ()

    def across(entries):
        return [
            (swap(array, 1), tuple((offsets, flip + 1) for offsets, flip in at))
            for array, at in entries
        ]

    for number in range(2, planes):
        value, where = arrival(number - 1)
        if number == 2:
            partials, value, passed = fence((partials, value, passed))
        else:
            value, passed, inputs = fence((value, passed, inputs))
        pieces += [(passed, passed_at)] + list(zip(near, near_at))
        todo += [(passed, passed_at)]
        moved = across(todo)
        near, near_at = [array for array, _ in moved], [at for _, at in moved]
        passed, passed_at = swap(value, 2), ((where, 2),)
        pieces += [(value, ((where, 0),))]
        todo = [(value, ((where, 0),))]
        if number + 1 == planes:
            moved = across(todo)
            near, near_at = near + [moved[0][0]], near_at + [moved[0][1]]
            todo = []
    pieces += list(zip(near, near_at)) + across(todo)
    inputs = [saved_input] + inputs
    last = (passed_at[0][0], 2)
    hidden = hidden_layers(grads, inputs, pieces, last, place)

    if fits:
        sums = met, None
    for step in range(2 if fits else 1, planes - 1):
        sums = reduce(step, sums)
    sums, hidden, passed = fence((sums, hidden, passed))
    total, rest = expert_results(
        grads, inputs, hidden, passed, swap(passed, 1), last, place, lookups, top
    )
    total, sums = fence((total, sums))
    if planes > 1:
        sums = reduce(planes - 1, sums)
    for back in others:
        value = rest[(back - 1) * tok : back * tok]
        total = total + over_expert(value, groups - back).astype(jnp.float32)
    sums = [partials[0]] + [came_in for came_in in sums[::-1] if came_in is not None]
    table = table_total(sums, lookups * part, half)
    return total.astype(jnp.bfloat16), table.reshape(lookups, part, width // ORDERS)


def solution(mesh):
    return jax.shard_map(
        per_device,
        mesh=mesh,
        in_specs=(
            P(("dp", "expert"), None),
            P(("dp", "expert"), None),
            P(("dp", "expert"), None),
            P(("dp", "expert"), None),
            P("expert", "dp", None),
            P("expert", "dp", None),
            P(("dp", "expert"), None),
            P(("dp", "expert"), None),
            P(("dp", "expert"), None),
        ),
        out_specs=(P(("dp", "expert"), None), P(None, ("dp", "expert"), None)),
        check_vma=False,
    )
```

```python
import functools
import math

import jax
import jax.numpy as jnp
from jax import lax
from jax.experimental import pallas as pl
from jax.experimental.pallas import tpu as pltpu
from jax.sharding import PartitionSpec as P

ORDERS = 2
SHARD = 128
LANES = 128


def silu_slope(pre):
    sig = jax.nn.sigmoid(pre)
    return sig * (1.0 + pre * (1.0 - sig))


def swap(value, bit):
    size = lax.axis_size("dp")
    return lax.ppermute(value, "dp", [(i, i ^ bit) for i in range(size)])


def over_expert(value, step):
    size = lax.axis_size("expert")
    return lax.ppermute(value, "expert", [(i, (i + step) % size) for i in range(size)])


def over_even(value):
    planes = lax.axis_size("dp") // 4
    pairs = []
    for z in range(1, planes - 1, 2):
        for i in range(z * 4, z * 4 + 4):
            pairs += [(i, i + 4), (i + 4, i)]
    return lax.ppermute(value, "dp", pairs)


def room(*arrays):
    return sum(math.prod(shape) * size for shape, size in arrays) + (2 << 20)


def pick(by_plane, plane):
    value = by_plane[-1]
    for z in range(len(by_plane) - 2, -1, -1):
        if by_plane[z] is not by_plane[z + 1]:
            value = jnp.where(plane <= z, by_plane[z], value)
    return value


def arrivals(planes):
    orders = []
    for z in range(planes):
        order = []
        for step in range(1, planes):
            for kind in (0, 1):
                offset = step if (z + kind) % 2 == 0 else -step
                if 0 <= z + offset < planes:
                    order.append((step, kind, offset))
        orders.append(order)
    return orders


def prepare_kernel(up_ref, down_ref, grad_ref, *refs):
    ids_ref, weights_ref, gate_ref, owner_ref, slot_ref, packed_ref, rows_ref, meta_ref = refs
    blocks, rows, cols = packed_ref.shape[1] // 2, packed_ref.shape[2], packed_ref.shape[3]
    for e in range(packed_ref.shape[0]):
        for b in range(blocks):
            packed_ref[e, b] = up_ref[e, b * rows : (b + 1) * rows, :]
            packed_ref[e, blocks + b] = down_ref[e, :, b * cols : (b + 1) * cols]
    tok, width = grad_ref.shape
    rows_ref[:, pl.ds(0, width)] = grad_ref[...]
    weights = weights_ref[...]
    high = weights.astype(jnp.bfloat16).astype(jnp.float32)
    meta_ref[...] = jnp.zeros_like(meta_ref)
    at = 0
    for value in (
        owner_ref[...].astype(jnp.float32),
        slot_ref[...].astype(jnp.float32),
        gate_ref[...],
        ids_ref[...].astype(jnp.float32),
        high,
        weights - high,
    ):
        meta_ref[pl.ds(at, value.shape[0]), :] = value
        at += value.shape[0]
    rows_ref[:, pl.ds(width, LANES)] = meta_ref[...].T.astype(jnp.bfloat16)


def prepare(up, down, grad_out, expert_ids, gate_weights, engram_gate, owner, slot):
    experts, _, hid = up.shape
    rows, width = down.shape[1:]
    tok = grad_out.shape[0]
    return pl.pallas_call(
        prepare_kernel,
        out_shape=(
            jax.ShapeDtypeStruct((experts, 2 * (width // hid), rows, hid), up.dtype),
            jax.ShapeDtypeStruct((tok, width + LANES), grad_out.dtype),
        ),
        scratch_shapes=[pltpu.VMEM((LANES, tok), jnp.float32)],
    )(up, down, grad_out, expert_ids.T, gate_weights.T, engram_gate.T, owner.T, slot.T)


def unstacked(refs):
    dims = min(ref.ndim for ref in refs)
    blocks = []
    for ref in refs:
        blocks += [ref] if ref.ndim == dims else [ref.at[i] for i in range(ref.shape[0])]
    return blocks


def folded(rows, width, shape):
    _, count, deep, wide = shape
    return (
        shape[0] == ORDERS
        and width % (wide // 2) == 0
        and rows % (2 * deep) == 0
        and (width // (wide // 2)) * (rows // (2 * deep)) == count
    )


def folds(rows, width, shape):
    _, _, deep, wide = shape
    for b in range(width // (wide // 2)):
        for h in range(rows // (2 * deep)):
            for u in range(2):
                yield (
                    b * (rows // (2 * deep)) + h,
                    u * (wide // 2),
                    (2 * h + u) * deep,
                    b * (wide // 2),
                )


def table_kernel(lookups, part, planes, offsets, place_ref, *refs):
    count = len(offsets)
    blocks = unstacked(refs[: -count - 2])
    outs, tokens, sem = refs[-count - 2 : -2], refs[-2], refs[-1]
    width = tokens.shape[1] - LANES
    half = width // ORDERS
    heads = lookups // ORDERS
    copies, at = [], 0
    for b, block in enumerate(blocks):
        copies.append(
            pltpu.make_async_copy(block, tokens.at[pl.ds(at, block.shape[0])], sem.at[b])
        )
        at += block.shape[0]
    for copy in copies:
        copy.start()
    for copy in copies:
        copy.wait()
    metas = [
        tokens[pl.ds(first, LANES), pl.ds(width, LANES)].astype(jnp.float32).T
        for first in range(0, at, LANES)
    ]
    meta = jnp.concatenate([m[: 3 * lookups] for m in metas], axis=1)
    key = meta[:lookups] * SHARD + meta[lookups : 2 * lookups]
    gate = meta[2 * lookups :]
    me, expert = place_ref[0], place_ref[1]
    plane = me // 4
    row = lax.broadcasted_iota(jnp.int32, (part, at), 0)
    size = heads * part
    for o in range(ORDERS):
        hits = []
        for offset in offsets:
            to = lax.rem(jnp.where(plane % 2 == 0, plane + offset, plane + planes - offset), planes)
            to = to * 4 + me % 4
            rows = (row + (to * SHARD + expert * part)).astype(jnp.float32)
            for j in range(o * heads, (o + 1) * heads):
                hit = jnp.where(rows == key[j : j + 1], gate[j : j + 1], 0.0)
                hits.append(hit.astype(jnp.bfloat16))
        sums = jnp.dot(
            jnp.concatenate(hits, axis=0),
            tokens[:, pl.ds(o * half, half)],
            preferred_element_type=jnp.float32,
        )
        for number, out in enumerate(outs):
            value = sums[number * size : (number + 1) * size].astype(out.dtype)
            if len(out.shape) == 2:
                out[pl.ds(o * size, size), :] = value
                continue
            deep, wide = out.shape[2], out.shape[3] // 2
            for block, lane, at, column in folds(size, half, out.shape):
                out[o, block, :, pl.ds(lane, wide)] = value[at : at + deep, column : column + wide]


def table_sums(blocks, place, lookups, part, offsets, shape):
    total = blocks[0].shape[1]
    planes = lax.axis_size("dp") // 4
    rows, half = lookups * part, (total - LANES) // ORDERS
    count = sum(block.shape[0] for block in blocks)
    return pl.pallas_call(
        functools.partial(table_kernel, lookups, part, planes, tuple(offsets)),
        out_shape=tuple(
            jax.ShapeDtypeStruct(shape, jnp.bfloat16 if offset else jnp.float32)
            for offset in offsets
        ),
        in_specs=[pl.BlockSpec(memory_space=pltpu.SMEM)]
        + [pl.BlockSpec(memory_space=pl.ANY)] * len(blocks),
        scratch_shapes=[
            pltpu.VMEM((count, total), jnp.bfloat16),
            pltpu.SemaphoreType.DMA((len(blocks),)),
        ],
        compiler_params=pltpu.CompilerParams(
            vmem_limit_bytes=room(
                ((count, total), 2), ((len(offsets) + 1, rows, half), 4), ((len(offsets), rows, count), 2)
            )
        ),
        cost_estimate=pl.CostEstimate(
            flops=2 * len(offsets) * rows * count * half,
            bytes_accessed=2 * count * total + 2 * len(offsets) * rows * half,
            transcendentals=0,
        ),
    )(place, *blocks)


def table_total_kernel(*refs):
    values, out = refs[:-1], refs[-1]
    if len(values[0].shape) == 2:
        out[...] = sum(value[...].astype(jnp.float32) for value in values)
        return
    size, width = out.shape[0] // ORDERS, out.shape[1]
    deep, wide = values[0].shape[2], values[0].shape[3] // 2
    for o in range(ORDERS):
        for block, lane, at, column in folds(size, width, values[0].shape):
            out[pl.ds(o * size + at, deep), pl.ds(column, wide)] = sum(
                value[o, block, :, pl.ds(lane, wide)].astype(jnp.float32) for value in values
            )


def table_total(values, rows, width):
    return pl.pallas_call(
        table_total_kernel,
        out_shape=jax.ShapeDtypeStruct((rows, width), jnp.float32),
        compiler_params=pltpu.CompilerParams(
            vmem_limit_bytes=room(((len(values) + 1, rows, width), 4))
        ),
    )(*values)


def located(where, place_ref, planes):
    offsets, flip = where
    me = place_ref[0]
    at = jnp.bitwise_xor(me, flip)
    for z, offset in enumerate(offsets):
        if offset:
            at = at + jnp.where(me // 4 == z, 4 * offset, 0)
    return at


def token_copies(tokens, targets, sem):
    groups = len(tokens) // 2
    tok = tokens[0].shape[0]
    copies = []
    for number, token in enumerate(tokens):
        target, g = targets[number // groups], number % groups
        copies.append(
            pltpu.make_async_copy(
                token, target.at[pl.ds(g * tok, tok)], sem.at[number // groups, g]
            )
        )
    return copies


def row_chunk(groups, tok):
    return 2 * tok if groups % 2 == 0 else tok


def hidden_kernel(where, last, groups, planes, *refs):
    place_ref, tokens, refs = refs[0], refs[1 : 1 + 2 * groups], refs[1 + 2 * groups :]
    pieces, refs = unstacked(refs[:-9]), refs[-9:]
    turned_ref, pre_ref, back_ref, grad, inp, up, down, token_sem, piece_sem = refs
    experts, blocks, size, rows, hid = down.shape
    copies = token_copies(tokens, (grad, inp), token_sem)
    for number, piece in enumerate(pieces):
        at = located(where[number], place_ref, planes)
        copies.append(
            pltpu.make_async_copy(
                piece.at[:, pl.ds(0, blocks)],
                up.at[:, pl.ds(at * blocks, blocks)],
                piece_sem.at[0, number],
            )
        )
        copies.append(
            pltpu.make_async_copy(
                piece.at[:, pl.ds(blocks, blocks)], down.at[:, :, at], piece_sem.at[1, number]
            )
        )
    for copy in copies:
        copy.start()
    for copy in copies:
        copy.wait()
    pair = located(last, place_ref, planes) // 2
    up[:, pl.ds(pair * 2 * blocks, 2 * blocks)] = jnp.zeros(
        (experts, 2 * blocks, rows, hid), up.dtype
    )
    tok = tokens[0].shape[0]
    chunk = row_chunk(groups, tok)
    for e in range(experts):
        for b in range(blocks):
            block = up[e, b * size : (b + 1) * size].reshape(size * rows, hid)
            turned_ref[e, :, pl.ds(b * hid, hid)] = block.T
    for start in range(0, groups * tok, chunk):
        span = pl.ds(start, chunk)
        for e in range(experts):
            pre = jnp.zeros((chunk, hid), jnp.float32)
            back = jnp.zeros((chunk, hid), jnp.float32)
            for b in range(blocks):
                cols = pl.ds(b * hid, hid)
                pre += jnp.dot(
                    inp[span, cols],
                    up[e, b * size : (b + 1) * size].reshape(size * rows, hid),
                    preferred_element_type=jnp.float32,
                )
                back += lax.dot_general(
                    grad[span, cols],
                    down[e, b].reshape(size * rows, hid),
                    (((1,), (1,)), ((), ())),
                    preferred_element_type=jnp.float32,
                )
            pre_ref[span, pl.ds(e * hid, hid)] = pre
            back_ref[span, pl.ds(e * hid, hid)] = back


def slab_of(blocks, rows):
    held = 2 * blocks * rows
    return held, -(-(LANES - math.gcd(held, LANES) + held) // LANES) * LANES


def result_kernel(last, begin, groups, planes, lookups, top, *refs):
    place_ref, tokens, refs = refs[0], refs[1 : 1 + 2 * groups], refs[1 + 2 * groups :]
    turned_ref, first_ref, second_ref, pre_ref, back_ref, out_ref, *refs = refs
    grad, part, up, down, turned, pre_part, back_part, token_sem, piece_sem, turned_sem = refs
    count, width = out_ref.shape
    tok = count // groups
    experts, blocks, per, rows, hid = down.shape
    expert = place_ref[1]
    pair = located(last, place_ref, planes) // 2
    held, slab = slab_of(blocks, rows)
    base = pl.multiple_of(pair * held // LANES * LANES, LANES)
    skip = lax.rem(pair * held, LANES)

    up[...] = jnp.zeros_like(up)
    copies = token_copies(
        list(tokens[:groups]) + [token.at[:, pl.ds(base, slab)] for token in tokens[groups:]],
        (grad, part),
        token_sem,
    )
    for number, piece in enumerate((first_ref, second_ref)):
        at = located((last[0], last[1] + number), place_ref, planes)
        copies.append(
            pltpu.make_async_copy(
                piece.at[:, pl.ds(0, blocks)],
                up.at[:, pl.ds(skip // rows + lax.rem(at, 2) * blocks, blocks)],
                piece_sem.at[0, number],
            )
        )
        copies.append(
            pltpu.make_async_copy(
                piece.at[:, pl.ds(blocks, blocks)],
                down.at[:, :, lax.rem(at, per)],
                piece_sem.at[1, number],
            )
        )
    mine = pl.ds(begin, count)
    copies.append(pltpu.make_async_copy(pre_ref.at[mine], pre_part, piece_sem.at[0, 2]))
    copies.append(pltpu.make_async_copy(back_ref.at[mine], back_part, piece_sem.at[1, 2]))
    turns = [
        pltpu.make_async_copy(
            turned_ref.at[:, :, pl.ds(b * hid, hid)],
            turned.at[:, :, pl.ds(b * hid, hid)],
            turned_sem.at[b],
        )
        for b in range(blocks)
    ]
    for copy in copies + turns:
        copy.start()
    for copy in copies:
        copy.wait()

    hid_slab = pl.multiple_of(pair * 2 // per * LANES, LANES)
    hid_skip = lax.rem(pair * 2, per) * rows
    chunk = row_chunk(groups, tok)
    at = 3 * lookups
    lane = lax.broadcasted_iota(jnp.int32, (chunk, slab), 1)
    lane = jnp.logical_and(lane >= skip, lane < skip + held)
    hid_lane = lax.broadcasted_iota(jnp.int32, (chunk, LANES), 1)
    hid_lane = jnp.logical_and(hid_lane >= hid_skip, hid_lane < hid_skip + 2 * rows)
    for start in range(0, groups * tok, chunk):
        span = pl.ds(start, chunk)
        meta = grad[span, pl.ds(width, LANES)].astype(jnp.float32)
        mine = jnp.where(lane, part[span, :].astype(jnp.float32), 0.0).astype(jnp.bfloat16)
        slopes = []
        for e in range(experts):
            units = pl.ds(e * hid, hid)
            pre = pre_part[span, units] + jnp.dot(
                mine, up[e].reshape(slab, hid), preferred_element_type=jnp.float32
            )
            late = jnp.zeros((chunk, LANES), jnp.float32)
            for b in range(blocks):
                late += lax.dot_general(
                    grad[span, pl.ds(b * hid, hid)],
                    down[e, b].reshape(LANES, hid),
                    (((1,), (1,)), ((), ())),
                    preferred_element_type=jnp.float32,
                )
            lanes = pl.ds(pl.multiple_of(e * hid + hid_slab, LANES), LANES)
            back_part[span, lanes] = jnp.where(hid_lane, late, back_part[span, lanes])
            weight = jnp.zeros((chunk, 1), jnp.float32)
            number = (expert * experts + e).astype(jnp.float32)
            for k in range(top):
                value = meta[:, at + top + k : at + top + k + 1]
                value += meta[:, at + 2 * top + k : at + 2 * top + k + 1]
                weight += jnp.where(meta[:, at + k : at + k + 1] == number, value, 0.0)
            slope = back_part[span, units] * silu_slope(pre) * weight
            slopes.append(slope.astype(jnp.bfloat16))
        for b in range(blocks):
            cols = pl.ds(b * hid, hid)
            if start == 0:
                turns[b].wait()
            total = jnp.zeros((chunk, hid), jnp.float32)
            for e in range(experts):
                total += jnp.dot(
                    slopes[e], turned[e, :, cols], preferred_element_type=jnp.float32
                )
            out_ref[span, cols] = total.astype(out_ref.dtype)
        late = jnp.zeros((chunk, slab), jnp.float32)
        for e in range(experts):
            late += lax.dot_general(
                slopes[e],
                up[e].reshape(slab, hid),
                (((1,), (1,)), ((), ())),
                preferred_element_type=jnp.float32,
            )
        cols = pl.ds(base, slab)
        known = out_ref[span, cols].astype(jnp.float32)
        out_ref[span, cols] = (known + late).astype(out_ref.dtype)


def hidden_layers(grads, inputs, pieces, last, place):
    groups = len(grads)
    tok, width = inputs[0].shape
    experts, blocks2, rows, hid = pieces[0][0].shape[-4:]
    blocks = blocks2 // 2
    dp = lax.axis_size("dp")
    where = tuple(entry for _, entries in pieces for entry in entries)
    any_space, vmem = pl.BlockSpec(memory_space=pl.ANY), pl.BlockSpec(memory_space=pltpu.VMEM)
    return pl.pallas_call(
        functools.partial(hidden_kernel, where, last, groups, dp // 4),
        out_shape=(
            jax.ShapeDtypeStruct((experts, hid, width), jnp.bfloat16),
            jax.ShapeDtypeStruct((groups * tok, experts * hid), jnp.float32),
            jax.ShapeDtypeStruct((groups * tok, experts * hid), jnp.float32),
        ),
        in_specs=[pl.BlockSpec(memory_space=pltpu.SMEM)]
        + [any_space] * (2 * groups + len(pieces)),
        out_specs=(vmem, vmem, vmem),
        scratch_shapes=[
            pltpu.VMEM((groups * tok, width + LANES), jnp.bfloat16),
            pltpu.VMEM((groups * tok, width), jnp.bfloat16),
            pltpu.VMEM((experts, dp * blocks, rows, hid), jnp.bfloat16),
            pltpu.VMEM((experts, blocks, dp, rows, hid), jnp.bfloat16),
            pltpu.SemaphoreType.DMA((2, groups)),
            pltpu.SemaphoreType.DMA((2, len(where))),
        ],
        compiler_params=pltpu.CompilerParams(
            vmem_limit_bytes=room(
                ((groups * tok, 2 * width + LANES), 2),
                ((3, experts, hid, width), 2),
                ((2, groups * tok, experts * hid), 4),
            )
        ),
        cost_estimate=pl.CostEstimate(
            flops=4 * groups * tok * width * hid * experts,
            bytes_accessed=6 * experts * width * hid + 8 * groups * tok * width,
            transcendentals=0,
        ),
    )(place, *grads, *inputs, *[piece[0] for piece in pieces])


def expert_results(grads, inputs, hidden, first, second, last, place, lookups, top, begin, dtype):
    groups = len(grads)
    tok, width = inputs[0].shape
    experts, blocks2, rows, hid = first.shape
    blocks = blocks2 // 2
    dp = lax.axis_size("dp")
    turned, pre, back = hidden
    slab = slab_of(blocks, rows)[1]
    any_space, vmem = pl.BlockSpec(memory_space=pl.ANY), pl.BlockSpec(memory_space=pltpu.VMEM)
    return pl.pallas_call(
        functools.partial(result_kernel, last, begin, groups, dp // 4, lookups, top),
        out_shape=jax.ShapeDtypeStruct((groups * tok, width), dtype),
        in_specs=[pl.BlockSpec(memory_space=pltpu.SMEM)] + [any_space] * (2 * groups + 5),
        out_specs=vmem,
        scratch_shapes=[
            pltpu.VMEM((groups * tok, width + LANES), jnp.bfloat16),
            pltpu.VMEM((groups * tok, slab), jnp.bfloat16),
            pltpu.VMEM((experts, slab // rows, rows, hid), jnp.bfloat16),
            pltpu.VMEM((experts, blocks, LANES // rows, rows, hid), jnp.bfloat16),
            pltpu.VMEM(turned.shape, jnp.bfloat16),
            pltpu.VMEM((groups * tok, pre.shape[1]), jnp.float32),
            pltpu.VMEM((groups * tok, pre.shape[1]), jnp.float32),
            pltpu.SemaphoreType.DMA((2, groups)),
            pltpu.SemaphoreType.DMA((2, 3)),
            pltpu.SemaphoreType.DMA((blocks,)),
        ],
        compiler_params=pltpu.CompilerParams(
            vmem_limit_bytes=room(
                ((groups * tok, width + LANES + slab), 2),
                ((experts, hid, width + slab), 2),
                ((experts, LANES, width), 2),
                ((2, groups * tok, experts * hid), 4),
                ((groups * tok, width), 4),
            )
        ),
        cost_estimate=pl.CostEstimate(
            flops=2 * groups * tok * width * hid * experts,
            bytes_accessed=2 * experts * width * hid + 12 * groups * tok * width,
            transcendentals=groups * tok * hid * experts,
        ),
    )(place, *grads, *inputs, turned, first, second, pre, back)


def per_device(
    grad_out,
    saved_input,
    expert_ids,
    gate_weights,
    up_weight,
    down_weight,
    engram_gate,
    memory_owner,
    memory_slot,
):
    tok, width = grad_out.shape
    lookups, top = engram_gate.shape[1], expert_ids.shape[1]
    groups = lax.axis_size("expert")
    planes = lax.axis_size("dp") // 4
    part = SHARD // groups
    me = lax.axis_index("dp")
    plane = me // 4
    place = jnp.stack([me, lax.axis_index("expert")]).astype(jnp.int32)
    others = range(1, groups)
    fence = lax.optimization_barrier

    packed, rows = prepare(
        up_weight,
        down_weight,
        grad_out,
        expert_ids,
        gate_weights,
        engram_gate,
        memory_owner,
        memory_slot,
    )
    orders = arrivals(planes)
    came = {}
    zero = (0,) * planes

    def along(step, line):
        even = over_even(line[0]) if step < planes - 1 else None
        return swap(line[1], 4), even

    def arrival(number):
        by_plane = [came[order[number][0]][order[number][1]] for order in orders]
        offsets = tuple(order[number][2] for order in orders)
        return pick(by_plane, plane), offsets

    def plus(share, came_in):
        return (share.astype(jnp.float32) + came_in.astype(jnp.float32)).astype(jnp.bfloat16)

    def reduce(step, sums):
        odd, even = partials[planes - step], partials[step]
        if step > 1 and sums[1] is not None:
            odd = plus(odd, sums[1])
        even = over_even(plus(even, sums[0])) if step > 1 else None
        return swap(odd, 4), even

    half = width // ORDERS
    fits = planes > 3 and folded(lookups // ORDERS * part, half, packed.shape)
    shape = packed.shape if fits else (lookups * part, half)


    rows_x = swap(rows, 2)
    got = [over_expert(rows, step) for step in others]
    came[1] = along(1, (packed, packed))
    late, rows_x = fence((packed, rows_x))
    rows_x, got, near = fence((rows_x, got, swap(rows, 1)))
    grads = [rows] + got
    far = [over_expert(rows_x, step) for step in others]
    near = [near, swap(rows_x, 1)]
    if planes > 2:
        came[2] = along(2, came[1])
        got, far = fence((got, far))
        near, came[2] = fence((near, came[2]))
    blocks = [rows, rows_x, *near, *got, *far]
    for block in got + far:
        blocks += [swap(block[: tok // 2], 1), swap(block[tok // 2 :], 1)]
    partials = table_sums(blocks, place, lookups, part, range(planes), shape)
    for step in range(3, planes - 1 if fits else planes):
        came[step] = along(step, came[step - 1])
    if fits:
        ends = jnp.logical_or(plane == 0, plane == planes - 1)
        met = swap(jnp.where(ends, partials[planes - 1], came[planes - 2][1]), 4)
        came[planes - 1] = (met, None)

    value, where = arrival(0)
    pair = jnp.stack([late, value])
    pair_x = swap(pair, 2)
    later, far = fence((saved_input, far))
    inputs = [over_expert(later, step) for step in others]

    pieces = [(pair, ((zero, 0), (where, 0)))]
    passed, passed_at = pair_x, ((zero, 2), (where, 2))
    todo, near, near_at = pieces[:1], [], []
    sums = ()

    def across(entries):
        return [
            (swap(array, 1), tuple((offsets, flip + 1) for offsets, flip in at))
            for array, at in entries
        ]

    for number in range(2, planes):
        value, where = arrival(number - 1)
        if number == 2:
            partials, value, passed = fence((partials, value, passed))
        else:
            value, passed, inputs = fence((value, passed, inputs))
        pieces += [(passed, passed_at)] + list(zip(near, near_at))
        todo += [(passed, passed_at)]
        moved = across(todo)
        near, near_at = [array for array, _ in moved], [at for _, at in moved]
        passed, passed_at = swap(value, 2), ((where, 2),)
        pieces += [(value, ((where, 0),))]
        todo = [(value, ((where, 0),))]
        if number + 1 == planes:
            moved = across(todo)
            near, near_at = near + [moved[0][0]], near_at + [moved[0][1]]
            todo = []
    pieces += list(zip(near, near_at)) + across(todo)
    inputs = [saved_input] + inputs
    last = (passed_at[0][0], 2)
    hidden = hidden_layers(grads, inputs, pieces, last, place)

    if fits:
        sums = met, None
    for step in range(2 if fits else 1, planes - 1):
        sums = reduce(step, sums)
    sums, hidden, passed = fence((sums, hidden, passed))
    first, second = passed, swap(passed, 1)

    def results(some, begin, dtype):
        return expert_results(
            [grads[g] for g in some],
            [inputs[g] for g in some],
            hidden,
            first,
            second,
            last,
            place,
            lookups,
            top,
            begin * tok,
            dtype,
        )

    if groups > 1:
        rest = results(others, 1, jnp.bfloat16)
        rest, sums = fence((rest, sums))
    if planes > 1:
        sums = reduce(planes - 1, sums)
    returned = [over_expert(rest[(k - 1) * tok : k * tok], groups - k) for k in others]
    total = results([0], 0, jnp.float32)
    for value in returned:
        total = total + value.astype(jnp.float32)
    sums = [partials[0]] + [came_in for came_in in sums[::-1] if came_in is not None]
    table = table_total(sums, lookups * part, half)
    return total.astype(jnp.bfloat16), table.reshape(lookups, part, width // ORDERS)


def solution(mesh):
    return jax.shard_map(
        per_device,
        mesh=mesh,
        in_specs=(
            P(("dp", "expert"), None),
            P(("dp", "expert"), None),
            P(("dp", "expert"), None),
            P(("dp", "expert"), None),
            P("expert", "dp", None),
            P("expert", "dp", None),
            P(("dp", "expert"), None),
            P(("dp", "expert"), None),
            P(("dp", "expert"), None),
        ),
        out_specs=(P(("dp", "expert"), None), P(None, ("dp", "expert"), None)),
        check_vma=False,
    )
```

```python
import functools
import math

import jax
import jax.numpy as jnp
from jax import lax
from jax.experimental import pallas as pl
from jax.experimental.pallas import tpu as pltpu
from jax.sharding import PartitionSpec as P

ORDERS = 2
SHARD = 128
LANES = 128


def silu_slope(pre):
    sig = jax.nn.sigmoid(pre)
    return sig * (1.0 + pre * (1.0 - sig))


def swap(value, bit):
    size = lax.axis_size("dp")
    return lax.ppermute(value, "dp", [(i, i ^ bit) for i in range(size)])


def over_expert(value, step):
    size = lax.axis_size("expert")
    return lax.ppermute(value, "expert", [(i, (i + step) % size) for i in range(size)])


def over_even(value):
    planes = lax.axis_size("dp") // 4
    pairs = []
    for z in range(1, planes - 1, 2):
        for i in range(z * 4, z * 4 + 4):
            pairs += [(i, i + 4), (i + 4, i)]
    return lax.ppermute(value, "dp", pairs)


def room(*arrays):
    return sum(math.prod(shape) * size for shape, size in arrays) + (2 << 20)


def pick(by_plane, plane):
    value = by_plane[-1]
    for z in range(len(by_plane) - 2, -1, -1):
        if by_plane[z] is not by_plane[z + 1]:
            value = jnp.where(plane <= z, by_plane[z], value)
    return value


def arrivals(planes):
    orders = []
    for z in range(planes):
        order = []
        for step in range(1, planes):
            for kind in (0, 1):
                offset = step if (z + kind) % 2 == 0 else -step
                if 0 <= z + offset < planes:
                    order.append((step, kind, offset))
        orders.append(order)
    return orders


def prepare_kernel(up_ref, down_ref, grad_ref, *refs):
    ids_ref, weights_ref, gate_ref, owner_ref, slot_ref, packed_ref, rows_ref, meta_ref = refs
    blocks, rows, cols = packed_ref.shape[1] // 2, packed_ref.shape[2], packed_ref.shape[3]
    for e in range(packed_ref.shape[0]):
        for b in range(blocks):
            packed_ref[e, b] = up_ref[e, b * rows : (b + 1) * rows, :]
            packed_ref[e, blocks + b] = down_ref[e, :, b * cols : (b + 1) * cols]
    tok, width = grad_ref.shape
    rows_ref[:, pl.ds(0, width)] = grad_ref[...]
    weights = weights_ref[...]
    high = weights.astype(jnp.bfloat16).astype(jnp.float32)
    meta_ref[...] = jnp.zeros_like(meta_ref)
    at = 0
    for value in (
        owner_ref[...].astype(jnp.float32),
        slot_ref[...].astype(jnp.float32),
        gate_ref[...],
        ids_ref[...].astype(jnp.float32),
        high,
        weights - high,
    ):
        meta_ref[pl.ds(at, value.shape[0]), :] = value
        at += value.shape[0]
    rows_ref[:, pl.ds(width, LANES)] = meta_ref[...].T.astype(jnp.bfloat16)


def prepare(up, down, grad_out, expert_ids, gate_weights, engram_gate, owner, slot):
    experts, _, hid = up.shape
    rows, width = down.shape[1:]
    tok = grad_out.shape[0]
    return pl.pallas_call(
        prepare_kernel,
        out_shape=(
            jax.ShapeDtypeStruct((experts, 2 * (width // hid), rows, hid), up.dtype),
            jax.ShapeDtypeStruct((tok, width + LANES), grad_out.dtype),
        ),
        scratch_shapes=[pltpu.VMEM((LANES, tok), jnp.float32)],
    )(up, down, grad_out, expert_ids.T, gate_weights.T, engram_gate.T, owner.T, slot.T)


def unstacked(refs):
    dims = min(ref.ndim for ref in refs)
    blocks = []
    for ref in refs:
        blocks += [ref] if ref.ndim == dims else [ref.at[i] for i in range(ref.shape[0])]
    return blocks


def folded(rows, width, shape):
    _, count, deep, wide = shape
    return (
        shape[0] == ORDERS
        and width % (wide // 2) == 0
        and rows % (2 * deep) == 0
        and (width // (wide // 2)) * (rows // (2 * deep)) == count
    )


def folds(rows, width, shape):
    _, _, deep, wide = shape
    for b in range(width // (wide // 2)):
        for h in range(rows // (2 * deep)):
            for u in range(2):
                yield (
                    b * (rows // (2 * deep)) + h,
                    u * (wide // 2),
                    (2 * h + u) * deep,
                    b * (wide // 2),
                )


def table_kernel(lookups, part, planes, offsets, place_ref, *refs):
    count = len(offsets)
    blocks = unstacked(refs[: -count - 2])
    outs, tokens, sem = refs[-count - 2 : -2], refs[-2], refs[-1]
    width = tokens.shape[1] - LANES
    half = width // ORDERS
    heads = lookups // ORDERS
    copies, at = [], 0
    for b, block in enumerate(blocks):
        copies.append(
            pltpu.make_async_copy(block, tokens.at[pl.ds(at, block.shape[0])], sem.at[b])
        )
        at += block.shape[0]
    for copy in copies:
        copy.start()
    for copy in copies:
        copy.wait()
    metas = [
        tokens[pl.ds(first, LANES), pl.ds(width, LANES)].astype(jnp.float32).T
        for first in range(0, at, LANES)
    ]
    meta = jnp.concatenate([m[: 3 * lookups] for m in metas], axis=1)
    key = meta[:lookups] * SHARD + meta[lookups : 2 * lookups]
    gate = meta[2 * lookups :]
    me, expert = place_ref[0], place_ref[1]
    plane = me // 4
    row = lax.broadcasted_iota(jnp.int32, (part, at), 0)
    size = heads * part
    for o in range(ORDERS):
        hits = []
        for offset in offsets:
            to = lax.rem(jnp.where(plane % 2 == 0, plane + offset, plane + planes - offset), planes)
            to = to * 4 + me % 4
            rows = (row + (to * SHARD + expert * part)).astype(jnp.float32)
            for j in range(o * heads, (o + 1) * heads):
                hit = jnp.where(rows == key[j : j + 1], gate[j : j + 1], 0.0)
                hits.append(hit.astype(jnp.bfloat16))
        sums = jnp.dot(
            jnp.concatenate(hits, axis=0),
            tokens[:, pl.ds(o * half, half)],
            preferred_element_type=jnp.float32,
        )
        for number, out in enumerate(outs):
            value = sums[number * size : (number + 1) * size].astype(out.dtype)
            if len(out.shape) == 2:
                out[pl.ds(o * size, size), :] = value
                continue
            deep, wide = out.shape[2], out.shape[3] // 2
            for block, lane, at, column in folds(size, half, out.shape):
                out[o, block, :, pl.ds(lane, wide)] = value[at : at + deep, column : column + wide]


def table_sums(blocks, place, lookups, part, offsets, shape):
    total = blocks[0].shape[1]
    planes = lax.axis_size("dp") // 4
    rows, half = lookups * part, (total - LANES) // ORDERS
    count = sum(block.shape[0] for block in blocks)
    return pl.pallas_call(
        functools.partial(table_kernel, lookups, part, planes, tuple(offsets)),
        out_shape=tuple(
            jax.ShapeDtypeStruct(shape, jnp.bfloat16 if offset else jnp.float32)
            for offset in offsets
        ),
        in_specs=[pl.BlockSpec(memory_space=pltpu.SMEM)]
        + [pl.BlockSpec(memory_space=pl.ANY)] * len(blocks),
        scratch_shapes=[
            pltpu.VMEM((count, total), jnp.bfloat16),
            pltpu.SemaphoreType.DMA((len(blocks),)),
        ],
        compiler_params=pltpu.CompilerParams(
            vmem_limit_bytes=room(
                ((count, total), 2), ((len(offsets) + 1, rows, half), 4), ((len(offsets), rows, count), 2)
            )
        ),
        cost_estimate=pl.CostEstimate(
            flops=2 * len(offsets) * rows * count * half,
            bytes_accessed=1 << 12,
            transcendentals=0,
        ),
    )(place, *blocks)


def table_total_kernel(*refs):
    values, out = refs[:-1], refs[-1]
    if len(values[0].shape) == 2:
        out[...] = sum(value[...].astype(jnp.float32) for value in values)
        return
    size, width = out.shape[0] // ORDERS, out.shape[1]
    deep, wide = values[0].shape[2], values[0].shape[3] // 2
    for o in range(ORDERS):
        for block, lane, at, column in folds(size, width, values[0].shape):
            out[pl.ds(o * size + at, deep), pl.ds(column, wide)] = sum(
                value[o, block, :, pl.ds(lane, wide)].astype(jnp.float32) for value in values
            )


def table_total(values, rows, width):
    return pl.pallas_call(
        table_total_kernel,
        out_shape=jax.ShapeDtypeStruct((rows, width), jnp.float32),
        compiler_params=pltpu.CompilerParams(
            vmem_limit_bytes=room(((len(values) + 1, rows, width), 4))
        ),
    )(*values)


def located(where, place_ref, planes):
    offsets, flip = where
    me = place_ref[0]
    at = jnp.bitwise_xor(me, flip)
    for z, offset in enumerate(offsets):
        if offset:
            at = at + jnp.where(me // 4 == z, 4 * offset, 0)
    return at


def token_copies(tokens, targets, sem):
    groups = len(tokens) // 2
    tok = tokens[0].shape[0]
    copies = []
    for number, token in enumerate(tokens):
        target, g = targets[number // groups], number % groups
        copies.append(
            pltpu.make_async_copy(
                token, target.at[pl.ds(g * tok, tok)], sem.at[number // groups, g]
            )
        )
    return copies


def row_chunk(groups, tok):
    return 2 * tok if groups % 2 == 0 else tok


def hidden_kernel(where, last, groups, planes, *refs):
    place_ref, tokens, refs = refs[0], refs[1 : 1 + 2 * groups], refs[1 + 2 * groups :]
    pieces, refs = unstacked(refs[:-9]), refs[-9:]
    turned_ref, pre_ref, back_ref, grad, inp, up, down, token_sem, piece_sem = refs
    experts, blocks, size, rows, hid = down.shape
    copies = token_copies(tokens, (grad, inp), token_sem)
    for number, piece in enumerate(pieces):
        at = located(where[number], place_ref, planes)
        copies.append(
            pltpu.make_async_copy(
                piece.at[:, pl.ds(0, blocks)],
                up.at[:, pl.ds(at * blocks, blocks)],
                piece_sem.at[0, number],
            )
        )
        copies.append(
            pltpu.make_async_copy(
                piece.at[:, pl.ds(blocks, blocks)], down.at[:, :, at], piece_sem.at[1, number]
            )
        )
    for copy in copies:
        copy.start()
    for copy in copies:
        copy.wait()
    pair = located(last, place_ref, planes) // 2
    up[:, pl.ds(pair * 2 * blocks, 2 * blocks)] = jnp.zeros(
        (experts, 2 * blocks, rows, hid), up.dtype
    )
    tok = tokens[0].shape[0]
    chunk = row_chunk(groups, tok)
    for e in range(experts):
        for b in range(blocks):
            block = up[e, b * size : (b + 1) * size].reshape(size * rows, hid)
            turned_ref[e, :, pl.ds(b * hid, hid)] = block.T
    for start in range(0, groups * tok, chunk):
        span = pl.ds(start, chunk)
        for e in range(experts):
            pre = jnp.zeros((chunk, hid), jnp.float32)
            back = jnp.zeros((chunk, hid), jnp.float32)
            for b in range(blocks):
                cols = pl.ds(b * hid, hid)
                pre += jnp.dot(
                    inp[span, cols],
                    up[e, b * size : (b + 1) * size].reshape(size * rows, hid),
                    preferred_element_type=jnp.float32,
                )
                back += lax.dot_general(
                    grad[span, cols],
                    down[e, b].reshape(size * rows, hid),
                    (((1,), (1,)), ((), ())),
                    preferred_element_type=jnp.float32,
                )
            pre_ref[span, pl.ds(e * hid, hid)] = pre
            back_ref[span, pl.ds(e * hid, hid)] = back


def slab_of(blocks, rows):
    held = 2 * blocks * rows
    return held, -(-(LANES - math.gcd(held, LANES) + held) // LANES) * LANES


def result_kernel(last, begin, groups, planes, lookups, top, *refs):
    place_ref, tokens, refs = refs[0], refs[1 : 1 + 2 * groups], refs[1 + 2 * groups :]
    turned_ref, first_ref, second_ref, pre_ref, back_ref, out_ref, *refs = refs
    grad, part, up, down, turned, pre_part, back_part, token_sem, piece_sem, turned_sem = refs
    count, width = out_ref.shape
    tok = count // groups
    experts, blocks, per, rows, hid = down.shape
    expert = place_ref[1]
    pair = located(last, place_ref, planes) // 2
    held, slab = slab_of(blocks, rows)
    base = pl.multiple_of(pair * held // LANES * LANES, LANES)
    skip = lax.rem(pair * held, LANES)

    up[...] = jnp.zeros_like(up)
    copies = token_copies(
        list(tokens[:groups]) + [token.at[:, pl.ds(base, slab)] for token in tokens[groups:]],
        (grad, part),
        token_sem,
    )
    for number, piece in enumerate((first_ref, second_ref)):
        at = located((last[0], last[1] + number), place_ref, planes)
        copies.append(
            pltpu.make_async_copy(
                piece.at[:, pl.ds(0, blocks)],
                up.at[:, pl.ds(skip // rows + lax.rem(at, 2) * blocks, blocks)],
                piece_sem.at[0, number],
            )
        )
        copies.append(
            pltpu.make_async_copy(
                piece.at[:, pl.ds(blocks, blocks)],
                down.at[:, :, lax.rem(at, per)],
                piece_sem.at[1, number],
            )
        )
    mine = pl.ds(begin, count)
    copies.append(pltpu.make_async_copy(pre_ref.at[mine], pre_part, piece_sem.at[0, 2]))
    copies.append(pltpu.make_async_copy(back_ref.at[mine], back_part, piece_sem.at[1, 2]))
    turns = [
        pltpu.make_async_copy(
            turned_ref.at[:, :, pl.ds(b * hid, hid)],
            turned.at[:, :, pl.ds(b * hid, hid)],
            turned_sem.at[b],
        )
        for b in range(blocks)
    ]
    for copy in copies + turns:
        copy.start()
    for copy in copies:
        copy.wait()

    hid_slab = pl.multiple_of(pair * 2 // per * LANES, LANES)
    hid_skip = lax.rem(pair * 2, per) * rows
    chunk = row_chunk(groups, tok)
    at = 3 * lookups
    lane = lax.broadcasted_iota(jnp.int32, (chunk, slab), 1)
    lane = jnp.logical_and(lane >= skip, lane < skip + held)
    hid_lane = lax.broadcasted_iota(jnp.int32, (chunk, LANES), 1)
    hid_lane = jnp.logical_and(hid_lane >= hid_skip, hid_lane < hid_skip + 2 * rows)
    for start in range(0, groups * tok, chunk):
        span = pl.ds(start, chunk)
        meta = grad[span, pl.ds(width, LANES)].astype(jnp.float32)
        mine = jnp.where(lane, part[span, :].astype(jnp.float32), 0.0).astype(jnp.bfloat16)
        slopes = []
        for e in range(experts):
            units = pl.ds(e * hid, hid)
            pre = pre_part[span, units] + jnp.dot(
                mine, up[e].reshape(slab, hid), preferred_element_type=jnp.float32
            )
            late = jnp.zeros((chunk, LANES), jnp.float32)
            for b in range(blocks):
                late += lax.dot_general(
                    grad[span, pl.ds(b * hid, hid)],
                    down[e, b].reshape(LANES, hid),
                    (((1,), (1,)), ((), ())),
                    preferred_element_type=jnp.float32,
                )
            lanes = pl.ds(pl.multiple_of(e * hid + hid_slab, LANES), LANES)
            back_part[span, lanes] = jnp.where(hid_lane, late, back_part[span, lanes])
            weight = jnp.zeros((chunk, 1), jnp.float32)
            number = (expert * experts + e).astype(jnp.float32)
            for k in range(top):
                value = meta[:, at + top + k : at + top + k + 1]
                value += meta[:, at + 2 * top + k : at + 2 * top + k + 1]
                weight += jnp.where(meta[:, at + k : at + k + 1] == number, value, 0.0)
            slope = back_part[span, units] * silu_slope(pre) * weight
            slopes.append(slope.astype(jnp.bfloat16))
        for b in range(blocks):
            cols = pl.ds(b * hid, hid)
            if start == 0:
                turns[b].wait()
            total = jnp.zeros((chunk, hid), jnp.float32)
            for e in range(experts):
                total += jnp.dot(
                    slopes[e], turned[e, :, cols], preferred_element_type=jnp.float32
                )
            out_ref[span, cols] = total.astype(out_ref.dtype)
        late = jnp.zeros((chunk, slab), jnp.float32)
        for e in range(experts):
            late += lax.dot_general(
                slopes[e],
                up[e].reshape(slab, hid),
                (((1,), (1,)), ((), ())),
                preferred_element_type=jnp.float32,
            )
        cols = pl.ds(base, slab)
        known = out_ref[span, cols].astype(jnp.float32)
        out_ref[span, cols] = (known + late).astype(out_ref.dtype)


def hidden_layers(grads, inputs, pieces, last, place):
    groups = len(grads)
    tok, width = inputs[0].shape
    experts, blocks2, rows, hid = pieces[0][0].shape[-4:]
    blocks = blocks2 // 2
    dp = lax.axis_size("dp")
    where = tuple(entry for _, entries in pieces for entry in entries)
    any_space, vmem = pl.BlockSpec(memory_space=pl.ANY), pl.BlockSpec(memory_space=pltpu.VMEM)
    return pl.pallas_call(
        functools.partial(hidden_kernel, where, last, groups, dp // 4),
        out_shape=(
            jax.ShapeDtypeStruct((experts, hid, width), jnp.bfloat16),
            jax.ShapeDtypeStruct((groups * tok, experts * hid), jnp.float32),
            jax.ShapeDtypeStruct((groups * tok, experts * hid), jnp.float32),
        ),
        in_specs=[pl.BlockSpec(memory_space=pltpu.SMEM)]
        + [any_space] * (2 * groups + len(pieces)),
        out_specs=(vmem, vmem, vmem),
        scratch_shapes=[
            pltpu.VMEM((groups * tok, width + LANES), jnp.bfloat16),
            pltpu.VMEM((groups * tok, width), jnp.bfloat16),
            pltpu.VMEM((experts, dp * blocks, rows, hid), jnp.bfloat16),
            pltpu.VMEM((experts, blocks, dp, rows, hid), jnp.bfloat16),
            pltpu.SemaphoreType.DMA((2, groups)),
            pltpu.SemaphoreType.DMA((2, len(where))),
        ],
        compiler_params=pltpu.CompilerParams(
            vmem_limit_bytes=room(
                ((groups * tok, 2 * width + LANES), 2),
                ((3, experts, hid, width), 2),
                ((2, groups * tok, experts * hid), 4),
            )
        ),
        cost_estimate=pl.CostEstimate(
            flops=4 * groups * tok * width * hid * experts,
            bytes_accessed=6 * experts * width * hid + 8 * groups * tok * width,
            transcendentals=0,
        ),
    )(place, *grads, *inputs, *[piece[0] for piece in pieces])


def expert_results(grads, inputs, hidden, first, second, last, place, lookups, top, begin, dtype):
    groups = len(grads)
    tok, width = inputs[0].shape
    experts, blocks2, rows, hid = first.shape
    blocks = blocks2 // 2
    dp = lax.axis_size("dp")
    turned, pre, back = hidden
    slab = slab_of(blocks, rows)[1]
    any_space, vmem = pl.BlockSpec(memory_space=pl.ANY), pl.BlockSpec(memory_space=pltpu.VMEM)
    return pl.pallas_call(
        functools.partial(result_kernel, last, begin, groups, dp // 4, lookups, top),
        out_shape=jax.ShapeDtypeStruct((groups * tok, width), dtype),
        in_specs=[pl.BlockSpec(memory_space=pltpu.SMEM)] + [any_space] * (2 * groups + 5),
        out_specs=vmem,
        scratch_shapes=[
            pltpu.VMEM((groups * tok, width + LANES), jnp.bfloat16),
            pltpu.VMEM((groups * tok, slab), jnp.bfloat16),
            pltpu.VMEM((experts, slab // rows, rows, hid), jnp.bfloat16),
            pltpu.VMEM((experts, blocks, LANES // rows, rows, hid), jnp.bfloat16),
            pltpu.VMEM(turned.shape, jnp.bfloat16),
            pltpu.VMEM((groups * tok, pre.shape[1]), jnp.float32),
            pltpu.VMEM((groups * tok, pre.shape[1]), jnp.float32),
            pltpu.SemaphoreType.DMA((2, groups)),
            pltpu.SemaphoreType.DMA((2, 3)),
            pltpu.SemaphoreType.DMA((blocks,)),
        ],
        compiler_params=pltpu.CompilerParams(
            vmem_limit_bytes=room(
                ((groups * tok, width + LANES + slab), 2),
                ((experts, hid, width + slab), 2),
                ((experts, LANES, width), 2),
                ((2, groups * tok, experts * hid), 4),
                ((groups * tok, width), 4),
            )
        ),
        cost_estimate=pl.CostEstimate(
            flops=2 * groups * tok * width * hid * experts,
            bytes_accessed=2 * experts * width * hid + 12 * groups * tok * width,
            transcendentals=groups * tok * hid * experts,
        ),
    )(place, *grads, *inputs, turned, first, second, pre, back)


def per_device(
    grad_out,
    saved_input,
    expert_ids,
    gate_weights,
    up_weight,
    down_weight,
    engram_gate,
    memory_owner,
    memory_slot,
):
    tok, width = grad_out.shape
    lookups, top = engram_gate.shape[1], expert_ids.shape[1]
    groups = lax.axis_size("expert")
    planes = lax.axis_size("dp") // 4
    part = SHARD // groups
    me = lax.axis_index("dp")
    plane = me // 4
    place = jnp.stack([me, lax.axis_index("expert")]).astype(jnp.int32)
    others = range(1, groups)
    fence = lax.optimization_barrier

    packed, rows = prepare(
        up_weight,
        down_weight,
        grad_out,
        expert_ids,
        gate_weights,
        engram_gate,
        memory_owner,
        memory_slot,
    )
    orders = arrivals(planes)
    came = {}
    zero = (0,) * planes

    def along(step, line):
        even = over_even(line[0]) if step < planes - 1 else None
        return swap(line[1], 4), even

    def arrival(number):
        by_plane = [came[order[number][0]][order[number][1]] for order in orders]
        offsets = tuple(order[number][2] for order in orders)
        return pick(by_plane, plane), offsets

    def plus(share, came_in):
        return (share.astype(jnp.float32) + came_in.astype(jnp.float32)).astype(jnp.bfloat16)

    def reduce(step, sums):
        odd, even = partials[planes - step], partials[step]
        if step > 1 and sums[1] is not None:
            odd = plus(odd, sums[1])
        even = over_even(plus(even, sums[0])) if step > 1 else None
        return swap(odd, 4), even

    half = width // ORDERS
    fits = planes > 3 and folded(lookups // ORDERS * part, half, packed.shape)
    shape = packed.shape if fits else (lookups * part, half)


    rows_x = swap(rows, 2)
    got = [over_expert(rows, step) for step in others]
    came[1] = along(1, (packed, packed))
    late, rows_x = fence((packed, rows_x))
    rows_x, got, near = fence((rows_x, got, swap(rows, 1)))
    grads = [rows] + got
    far = [over_expert(rows_x, step) for step in others]
    near = [near, swap(rows_x, 1)]
    if planes > 2:
        came[2] = along(2, came[1])
        got, far = fence((got, far))
        near, came[2] = fence((near, came[2]))
    blocks = [rows, rows_x, *near, *got, *far]
    for block in got + far:
        blocks += [swap(block[: tok // 2], 1), swap(block[tok // 2 :], 1)]
    partials = table_sums(blocks, place, lookups, part, range(planes), shape)
    for step in range(3, planes - 1 if fits else planes):
        came[step] = along(step, came[step - 1])
    if fits:
        ends = jnp.logical_or(plane == 0, plane == planes - 1)
        met = swap(jnp.where(ends, partials[planes - 1], came[planes - 2][1]), 4)
        came[planes - 1] = (met, None)

    value, where = arrival(0)
    pair = jnp.stack([late, value])
    pair_x = swap(pair, 2)
    later, far = fence((saved_input, far))
    inputs = [over_expert(later, step) for step in others]

    pieces = [(pair, ((zero, 0), (where, 0)))]
    passed, passed_at = pair_x, ((zero, 2), (where, 2))
    todo, near, near_at = pieces[:1], [], []
    sums = ()

    def across(entries):
        return [
            (swap(array, 1), tuple((offsets, flip + 1) for offsets, flip in at))
            for array, at in entries
        ]

    for number in range(2, planes):
        value, where = arrival(number - 1)
        if number == 2:
            partials, value, passed = fence((partials, value, passed))
        else:
            value, passed, inputs = fence((value, passed, inputs))
        pieces += [(passed, passed_at)] + list(zip(near, near_at))
        todo += [(passed, passed_at)]
        moved = across(todo)
        near, near_at = [array for array, _ in moved], [at for _, at in moved]
        passed, passed_at = swap(value, 2), ((where, 2),)
        pieces += [(value, ((where, 0),))]
        todo = [(value, ((where, 0),))]
        if number + 1 == planes:
            moved = across(todo)
            near, near_at = near + [moved[0][0]], near_at + [moved[0][1]]
            todo = []
    pieces += list(zip(near, near_at)) + across(todo)
    inputs = [saved_input] + inputs
    last = (passed_at[0][0], 2)
    hidden = hidden_layers(grads, inputs, pieces, last, place)

    if fits:
        sums = met, None
    for step in range(2 if fits else 1, planes - 1):
        sums = reduce(step, sums)
    sums, hidden, passed = fence((sums, hidden, passed))
    first, second = passed, swap(passed, 1)

    def results(some, begin, dtype):
        return expert_results(
            [grads[g] for g in some],
            [inputs[g] for g in some],
            hidden,
            first,
            second,
            last,
            place,
            lookups,
            top,
            begin * tok,
            dtype,
        )

    if groups > 1:
        rest = results(others, 1, jnp.bfloat16)
        rest, sums = fence((rest, sums))
    if planes > 1:
        sums = reduce(planes - 1, sums)
    returned = [over_expert(rest[(k - 1) * tok : k * tok], groups - k) for k in others]
    total = results([0], 0, jnp.float32)
    for value in returned:
        total = total + value.astype(jnp.float32)
    sums = [partials[0]] + [came_in for came_in in sums[::-1] if came_in is not None]
    table = table_total(sums, lookups * part, half)
    return total.astype(jnp.bfloat16), table.reshape(lookups, part, width // ORDERS)


def solution(mesh):
    return jax.shard_map(
        per_device,
        mesh=mesh,
        in_specs=(
            P(("dp", "expert"), None),
            P(("dp", "expert"), None),
            P(("dp", "expert"), None),
            P(("dp", "expert"), None),
            P("expert", "dp", None),
            P("expert", "dp", None),
            P(("dp", "expert"), None),
            P(("dp", "expert"), None),
            P(("dp", "expert"), None),
        ),
        out_specs=(P(("dp", "expert"), None), P(None, ("dp", "expert"), None)),
        check_vma=False,
    )
```

```python
import functools
import math

import jax
import jax.numpy as jnp
from jax import lax
from jax.experimental import pallas as pl
from jax.experimental.pallas import tpu as pltpu
from jax.sharding import PartitionSpec as P

ORDERS = 2
SHARD = 128
LANES = 128


def silu_slope(pre):
    sig = jax.nn.sigmoid(pre)
    return sig * (1.0 + pre * (1.0 - sig))


def swap(value, bit):
    size = lax.axis_size("dp")
    return lax.ppermute(value, "dp", [(i, i ^ bit) for i in range(size)])


def over_expert(value, step):
    size = lax.axis_size("expert")
    return lax.ppermute(value, "expert", [(i, (i + step) % size) for i in range(size)])


def over_even(value):
    planes = lax.axis_size("dp") // 4
    pairs = []
    for z in range(1, planes - 1, 2):
        for i in range(z * 4, z * 4 + 4):
            pairs += [(i, i + 4), (i + 4, i)]
    return lax.ppermute(value, "dp", pairs)


def room(*arrays):
    return sum(math.prod(shape) * size for shape, size in arrays) + (2 << 20)


def pick(by_plane, plane):
    value = by_plane[-1]
    for z in range(len(by_plane) - 2, -1, -1):
        if by_plane[z] is not by_plane[z + 1]:
            value = jnp.where(plane <= z, by_plane[z], value)
    return value


def arrivals(planes):
    orders = []
    for z in range(planes):
        order = []
        for step in range(1, planes):
            for kind in (0, 1):
                offset = step if (z + kind) % 2 == 0 else -step
                if 0 <= z + offset < planes:
                    order.append((step, kind, offset))
        orders.append(order)
    return orders


def prepare_kernel(up_ref, down_ref, grad_ref, *refs):
    ids_ref, weights_ref, gate_ref, owner_ref, slot_ref, packed_ref, rows_ref, meta_ref = refs
    blocks, rows, cols = packed_ref.shape[1] // 2, packed_ref.shape[2], packed_ref.shape[3]
    for e in range(packed_ref.shape[0]):
        for b in range(blocks):
            packed_ref[e, b] = up_ref[e, b * rows : (b + 1) * rows, :]
            packed_ref[e, blocks + b] = down_ref[e, :, b * cols : (b + 1) * cols]
    tok, width = grad_ref.shape
    rows_ref[:, pl.ds(0, width)] = grad_ref[...]
    weights = weights_ref[...]
    high = weights.astype(jnp.bfloat16).astype(jnp.float32)
    meta_ref[...] = jnp.zeros_like(meta_ref)
    at = 0
    for value in (
        owner_ref[...].astype(jnp.float32),
        slot_ref[...].astype(jnp.float32),
        gate_ref[...],
        ids_ref[...].astype(jnp.float32),
        high,
        weights - high,
    ):
        meta_ref[pl.ds(at, value.shape[0]), :] = value
        at += value.shape[0]
    rows_ref[:, pl.ds(width, LANES)] = meta_ref[...].T.astype(jnp.bfloat16)


def prepare(up, down, grad_out, expert_ids, gate_weights, engram_gate, owner, slot):
    experts, _, hid = up.shape
    rows, width = down.shape[1:]
    tok = grad_out.shape[0]
    return pl.pallas_call(
        prepare_kernel,
        out_shape=(
            jax.ShapeDtypeStruct((experts, 2 * (width // hid), rows, hid), up.dtype),
            jax.ShapeDtypeStruct((tok, width + LANES), grad_out.dtype),
        ),
        scratch_shapes=[pltpu.VMEM((LANES, tok), jnp.float32)],
    )(up, down, grad_out, expert_ids.T, gate_weights.T, engram_gate.T, owner.T, slot.T)


def unstacked(refs):
    dims = min(ref.ndim for ref in refs)
    blocks = []
    for ref in refs:
        blocks += [ref] if ref.ndim == dims else [ref.at[i] for i in range(ref.shape[0])]
    return blocks


def folded(rows, width, shape):
    _, count, deep, wide = shape
    return (
        shape[0] == ORDERS
        and width % (wide // 2) == 0
        and rows % (2 * deep) == 0
        and (width // (wide // 2)) * (rows // (2 * deep)) == count
    )


def folds(rows, width, shape):
    _, _, deep, wide = shape
    for b in range(width // (wide // 2)):
        for h in range(rows // (2 * deep)):
            for u in range(2):
                yield (
                    b * (rows // (2 * deep)) + h,
                    u * (wide // 2),
                    (2 * h + u) * deep,
                    b * (wide // 2),
                )


def table_kernel(lookups, part, planes, offsets, place_ref, *refs):
    count = len(offsets)
    blocks = unstacked(refs[: -count - 3])
    outs, tokens, routing, sem = refs[-count - 3 : -3], refs[-3], refs[-2], refs[-1]
    width = tokens.shape[1]
    half = width // ORDERS
    heads = lookups // ORDERS
    firsts, copies, at = [], [], 0
    for b, block in enumerate(blocks):
        span = pl.ds(at, block.shape[0])
        firsts.append(
            pltpu.make_async_copy(
                block.at[:, pl.ds(width, LANES)], routing.at[span], sem.at[0, b]
            )
        )
        copies.append(
            pltpu.make_async_copy(block.at[:, pl.ds(0, width)], tokens.at[span], sem.at[1, b])
        )
        at += block.shape[0]
    for copy in firsts + copies:
        copy.start()
    for copy in firsts:
        copy.wait()
    metas = [
        routing[pl.ds(first, LANES), :].astype(jnp.float32).T for first in range(0, at, LANES)
    ]
    meta = jnp.concatenate([m[: 3 * lookups] for m in metas], axis=1)
    key = meta[:lookups] * SHARD + meta[lookups : 2 * lookups]
    gate = meta[2 * lookups :]
    me, expert = place_ref[0], place_ref[1]
    plane = me // 4
    row = lax.broadcasted_iota(jnp.int32, (part, at), 0)
    size = heads * part
    hits = []
    for o in range(ORDERS):
        for offset in offsets:
            to = lax.rem(jnp.where(plane % 2 == 0, plane + offset, plane + planes - offset), planes)
            to = to * 4 + me % 4
            rows = (row + (to * SHARD + expert * part)).astype(jnp.float32)
            for j in range(o * heads, (o + 1) * heads):
                hit = jnp.where(rows == key[j : j + 1], gate[j : j + 1], 0.0)
                hits.append(hit.astype(jnp.bfloat16))
    for copy in copies:
        copy.wait()
    for o in range(ORDERS):
        mine = hits[o * heads * count : (o + 1) * heads * count]
        sums = jnp.dot(
            jnp.concatenate(mine, axis=0),
            tokens[:, pl.ds(o * half, half)],
            preferred_element_type=jnp.float32,
        )
        for number, out in enumerate(outs):
            value = sums[number * size : (number + 1) * size].astype(out.dtype)
            if len(out.shape) == 2:
                out[pl.ds(o * size, size), :] = value
                continue
            deep, wide = out.shape[2], out.shape[3] // 2
            for block, lane, at, column in folds(size, half, out.shape):
                out[o, block, :, pl.ds(lane, wide)] = value[at : at + deep, column : column + wide]


def table_sums(blocks, place, lookups, part, offsets, shape):
    total = blocks[0].shape[1]
    planes = lax.axis_size("dp") // 4
    rows, half = lookups * part, (total - LANES) // ORDERS
    count = sum(block.shape[0] for block in blocks)
    return pl.pallas_call(
        functools.partial(table_kernel, lookups, part, planes, tuple(offsets)),
        out_shape=tuple(
            jax.ShapeDtypeStruct(shape, jnp.bfloat16 if offset else jnp.float32)
            for offset in offsets
        ),
        in_specs=[pl.BlockSpec(memory_space=pltpu.SMEM)]
        + [pl.BlockSpec(memory_space=pl.ANY)] * len(blocks),
        scratch_shapes=[
            pltpu.VMEM((count, total - LANES), jnp.bfloat16),
            pltpu.VMEM((count, LANES), jnp.bfloat16),
            pltpu.SemaphoreType.DMA((2, len(blocks))),
        ],
        compiler_params=pltpu.CompilerParams(
            vmem_limit_bytes=room(
                ((count, total), 2), ((len(offsets) + 1, rows, half), 4), ((len(offsets), rows, count), 2)
            )
        ),
        cost_estimate=pl.CostEstimate(
            flops=2 * len(offsets) * rows * count * half,
            bytes_accessed=1 << 12,
            transcendentals=0,
        ),
    )(place, *blocks)


def table_total_kernel(*refs):
    values, out = refs[:-1], refs[-1]
    if len(values[0].shape) == 2:
        out[...] = sum(value[...].astype(jnp.float32) for value in values)
        return
    size, width = out.shape[0] // ORDERS, out.shape[1]
    deep, wide = values[0].shape[2], values[0].shape[3] // 2
    for o in range(ORDERS):
        for block, lane, at, column in folds(size, width, values[0].shape):
            out[pl.ds(o * size + at, deep), pl.ds(column, wide)] = sum(
                value[o, block, :, pl.ds(lane, wide)].astype(jnp.float32) for value in values
            )


def table_total(values, rows, width):
    return pl.pallas_call(
        table_total_kernel,
        out_shape=jax.ShapeDtypeStruct((rows, width), jnp.float32),
        compiler_params=pltpu.CompilerParams(
            vmem_limit_bytes=room(((len(values) + 1, rows, width), 4))
        ),
    )(*values)


def located(where, place_ref, planes):
    offsets, flip = where
    me = place_ref[0]
    at = jnp.bitwise_xor(me, flip)
    for z, offset in enumerate(offsets):
        if offset:
            at = at + jnp.where(me // 4 == z, 4 * offset, 0)
    return at


def token_copies(tokens, targets, sem):
    groups = len(tokens) // 2
    tok = tokens[0].shape[0]
    copies = []
    for number, token in enumerate(tokens):
        target, g = targets[number // groups], number % groups
        copies.append(
            pltpu.make_async_copy(
                token, target.at[pl.ds(g * tok, tok)], sem.at[number // groups, g]
            )
        )
    return copies


def row_chunk(groups, tok):
    return 2 * tok if groups % 2 == 0 else tok


def hidden_kernel(where, last, groups, planes, *refs):
    place_ref, tokens, refs = refs[0], refs[1 : 1 + 2 * groups], refs[1 + 2 * groups :]
    pieces, refs = unstacked(refs[:-9]), refs[-9:]
    turned_ref, pre_ref, back_ref, grad, inp, up, down, token_sem, piece_sem = refs
    experts, blocks, size, rows, hid = down.shape
    copies = token_copies(tokens, (grad, inp), token_sem)
    for number, piece in enumerate(pieces):
        at = located(where[number], place_ref, planes)
        copies.append(
            pltpu.make_async_copy(
                piece.at[:, pl.ds(0, blocks)],
                up.at[:, pl.ds(at * blocks, blocks)],
                piece_sem.at[0, number],
            )
        )
        copies.append(
            pltpu.make_async_copy(
                piece.at[:, pl.ds(blocks, blocks)], down.at[:, :, at], piece_sem.at[1, number]
            )
        )
    for copy in copies:
        copy.start()
    for copy in copies:
        copy.wait()
    pair = located(last, place_ref, planes) // 2
    up[:, pl.ds(pair * 2 * blocks, 2 * blocks)] = jnp.zeros(
        (experts, 2 * blocks, rows, hid), up.dtype
    )
    tok = tokens[0].shape[0]
    chunk = row_chunk(groups, tok)
    for e in range(experts):
        for b in range(blocks):
            block = up[e, b * size : (b + 1) * size].reshape(size * rows, hid)
            turned_ref[e, :, pl.ds(b * hid, hid)] = block.T
    for start in range(0, groups * tok, chunk):
        span = pl.ds(start, chunk)
        for e in range(experts):
            pre = jnp.zeros((chunk, hid), jnp.float32)
            back = jnp.zeros((chunk, hid), jnp.float32)
            for b in range(blocks):
                cols = pl.ds(b * hid, hid)
                pre += jnp.dot(
                    inp[span, cols],
                    up[e, b * size : (b + 1) * size].reshape(size * rows, hid),
                    preferred_element_type=jnp.float32,
                )
                back += lax.dot_general(
                    grad[span, cols],
                    down[e, b].reshape(size * rows, hid),
                    (((1,), (1,)), ((), ())),
                    preferred_element_type=jnp.float32,
                )
            pre_ref[span, pl.ds(e * hid, hid)] = pre
            back_ref[span, pl.ds(e * hid, hid)] = back


def slab_of(blocks, rows):
    held = 2 * blocks * rows
    return held, -(-(LANES - math.gcd(held, LANES) + held) // LANES) * LANES


def result_kernel(last, begin, groups, planes, lookups, top, *refs):
    place_ref, tokens, refs = refs[0], refs[1 : 1 + 2 * groups], refs[1 + 2 * groups :]
    turned_ref, first_ref, second_ref, pre_ref, back_ref, out_ref, *refs = refs
    grad, part, up, down, turned, pre_part, back_part, token_sem, piece_sem, turned_sem = refs
    count, width = out_ref.shape
    tok = count // groups
    experts, blocks, per, rows, hid = down.shape
    expert = place_ref[1]
    pair = located(last, place_ref, planes) // 2
    held, slab = slab_of(blocks, rows)
    base = pl.multiple_of(pair * held // LANES * LANES, LANES)
    skip = lax.rem(pair * held, LANES)

    up[...] = jnp.zeros_like(up)
    copies = token_copies(
        list(tokens[:groups]) + [token.at[:, pl.ds(base, slab)] for token in tokens[groups:]],
        (grad, part),
        token_sem,
    )
    for number, piece in enumerate((first_ref, second_ref)):
        at = located((last[0], last[1] + number), place_ref, planes)
        copies.append(
            pltpu.make_async_copy(
                piece.at[:, pl.ds(0, blocks)],
                up.at[:, pl.ds(skip // rows + lax.rem(at, 2) * blocks, blocks)],
                piece_sem.at[0, number],
            )
        )
        copies.append(
            pltpu.make_async_copy(
                piece.at[:, pl.ds(blocks, blocks)],
                down.at[:, :, lax.rem(at, per)],
                piece_sem.at[1, number],
            )
        )
    mine = pl.ds(begin, count)
    copies.append(pltpu.make_async_copy(pre_ref.at[mine], pre_part, piece_sem.at[0, 2]))
    copies.append(pltpu.make_async_copy(back_ref.at[mine], back_part, piece_sem.at[1, 2]))
    turns = [
        pltpu.make_async_copy(
            turned_ref.at[:, :, pl.ds(b * hid, hid)],
            turned.at[:, :, pl.ds(b * hid, hid)],
            turned_sem.at[b],
        )
        for b in range(blocks)
    ]
    for copy in copies + turns:
        copy.start()
    for copy in copies:
        copy.wait()

    hid_slab = pl.multiple_of(pair * 2 // per * LANES, LANES)
    hid_skip = lax.rem(pair * 2, per) * rows
    chunk = row_chunk(groups, tok)
    at = 3 * lookups
    lane = lax.broadcasted_iota(jnp.int32, (chunk, slab), 1)
    lane = jnp.logical_and(lane >= skip, lane < skip + held)
    hid_lane = lax.broadcasted_iota(jnp.int32, (chunk, LANES), 1)
    hid_lane = jnp.logical_and(hid_lane >= hid_skip, hid_lane < hid_skip + 2 * rows)
    for start in range(0, groups * tok, chunk):
        span = pl.ds(start, chunk)
        meta = grad[span, pl.ds(width, LANES)].astype(jnp.float32)
        mine = jnp.where(lane, part[span, :].astype(jnp.float32), 0.0).astype(jnp.bfloat16)
        slopes = []
        for e in range(experts):
            units = pl.ds(e * hid, hid)
            pre = pre_part[span, units] + jnp.dot(
                mine, up[e].reshape(slab, hid), preferred_element_type=jnp.float32
            )
            late = jnp.zeros((chunk, LANES), jnp.float32)
            for b in range(blocks):
                late += lax.dot_general(
                    grad[span, pl.ds(b * hid, hid)],
                    down[e, b].reshape(LANES, hid),
                    (((1,), (1,)), ((), ())),
                    preferred_element_type=jnp.float32,
                )
            lanes = pl.ds(pl.multiple_of(e * hid + hid_slab, LANES), LANES)
            back_part[span, lanes] = jnp.where(hid_lane, late, back_part[span, lanes])
            weight = jnp.zeros((chunk, 1), jnp.float32)
            number = (expert * experts + e).astype(jnp.float32)
            for k in range(top):
                value = meta[:, at + top + k : at + top + k + 1]
                value += meta[:, at + 2 * top + k : at + 2 * top + k + 1]
                weight += jnp.where(meta[:, at + k : at + k + 1] == number, value, 0.0)
            slope = back_part[span, units] * silu_slope(pre) * weight
            slopes.append(slope.astype(jnp.bfloat16))
        for b in range(blocks):
            cols = pl.ds(b * hid, hid)
            if start == 0:
                turns[b].wait()
            total = jnp.zeros((chunk, hid), jnp.float32)
            for e in range(experts):
                total += jnp.dot(
                    slopes[e], turned[e, :, cols], preferred_element_type=jnp.float32
                )
            out_ref[span, cols] = total.astype(out_ref.dtype)
        late = jnp.zeros((chunk, slab), jnp.float32)
        for e in range(experts):
            late += lax.dot_general(
                slopes[e],
                up[e].reshape(slab, hid),
                (((1,), (1,)), ((), ())),
                preferred_element_type=jnp.float32,
            )
        cols = pl.ds(base, slab)
        known = out_ref[span, cols].astype(jnp.float32)
        out_ref[span, cols] = (known + late).astype(out_ref.dtype)


def hidden_layers(grads, inputs, pieces, last, place):
    groups = len(grads)
    tok, width = inputs[0].shape
    experts, blocks2, rows, hid = pieces[0][0].shape[-4:]
    blocks = blocks2 // 2
    dp = lax.axis_size("dp")
    where = tuple(entry for _, entries in pieces for entry in entries)
    any_space, vmem = pl.BlockSpec(memory_space=pl.ANY), pl.BlockSpec(memory_space=pltpu.VMEM)
    return pl.pallas_call(
        functools.partial(hidden_kernel, where, last, groups, dp // 4),
        out_shape=(
            jax.ShapeDtypeStruct((experts, hid, width), jnp.bfloat16),
            jax.ShapeDtypeStruct((groups * tok, experts * hid), jnp.float32),
            jax.ShapeDtypeStruct((groups * tok, experts * hid), jnp.float32),
        ),
        in_specs=[pl.BlockSpec(memory_space=pltpu.SMEM)]
        + [any_space] * (2 * groups + len(pieces)),
        out_specs=(vmem, vmem, vmem),
        scratch_shapes=[
            pltpu.VMEM((groups * tok, width + LANES), jnp.bfloat16),
            pltpu.VMEM((groups * tok, width), jnp.bfloat16),
            pltpu.VMEM((experts, dp * blocks, rows, hid), jnp.bfloat16),
            pltpu.VMEM((experts, blocks, dp, rows, hid), jnp.bfloat16),
            pltpu.SemaphoreType.DMA((2, groups)),
            pltpu.SemaphoreType.DMA((2, len(where))),
        ],
        compiler_params=pltpu.CompilerParams(
            vmem_limit_bytes=room(
                ((groups * tok, 2 * width + LANES), 2),
                ((3, experts, hid, width), 2),
                ((2, groups * tok, experts * hid), 4),
            )
        ),
        cost_estimate=pl.CostEstimate(
            flops=4 * groups * tok * width * hid * experts,
            bytes_accessed=6 * experts * width * hid + 8 * groups * tok * width,
            transcendentals=0,
        ),
    )(place, *grads, *inputs, *[piece[0] for piece in pieces])


def expert_results(grads, inputs, hidden, first, second, last, place, lookups, top, begin, dtype):
    groups = len(grads)
    tok, width = inputs[0].shape
    experts, blocks2, rows, hid = first.shape
    blocks = blocks2 // 2
    dp = lax.axis_size("dp")
    turned, pre, back = hidden
    slab = slab_of(blocks, rows)[1]
    any_space, vmem = pl.BlockSpec(memory_space=pl.ANY), pl.BlockSpec(memory_space=pltpu.VMEM)
    return pl.pallas_call(
        functools.partial(result_kernel, last, begin, groups, dp // 4, lookups, top),
        out_shape=jax.ShapeDtypeStruct((groups * tok, width), dtype),
        in_specs=[pl.BlockSpec(memory_space=pltpu.SMEM)] + [any_space] * (2 * groups + 5),
        out_specs=vmem,
        scratch_shapes=[
            pltpu.VMEM((groups * tok, width + LANES), jnp.bfloat16),
            pltpu.VMEM((groups * tok, slab), jnp.bfloat16),
            pltpu.VMEM((experts, slab // rows, rows, hid), jnp.bfloat16),
            pltpu.VMEM((experts, blocks, LANES // rows, rows, hid), jnp.bfloat16),
            pltpu.VMEM(turned.shape, jnp.bfloat16),
            pltpu.VMEM((groups * tok, pre.shape[1]), jnp.float32),
            pltpu.VMEM((groups * tok, pre.shape[1]), jnp.float32),
            pltpu.SemaphoreType.DMA((2, groups)),
            pltpu.SemaphoreType.DMA((2, 3)),
            pltpu.SemaphoreType.DMA((blocks,)),
        ],
        compiler_params=pltpu.CompilerParams(
            vmem_limit_bytes=room(
                ((groups * tok, width + LANES + slab), 2),
                ((experts, hid, width + slab), 2),
                ((experts, LANES, width), 2),
                ((2, groups * tok, experts * hid), 4),
                ((groups * tok, width), 4),
            )
        ),
        cost_estimate=pl.CostEstimate(
            flops=2 * groups * tok * width * hid * experts,
            bytes_accessed=2 * experts * width * hid + 12 * groups * tok * width,
            transcendentals=groups * tok * hid * experts,
        ),
    )(place, *grads, *inputs, turned, first, second, pre, back)


def per_device(
    grad_out,
    saved_input,
    expert_ids,
    gate_weights,
    up_weight,
    down_weight,
    engram_gate,
    memory_owner,
    memory_slot,
):
    tok, width = grad_out.shape
    lookups, top = engram_gate.shape[1], expert_ids.shape[1]
    groups = lax.axis_size("expert")
    planes = lax.axis_size("dp") // 4
    part = SHARD // groups
    me = lax.axis_index("dp")
    plane = me // 4
    place = jnp.stack([me, lax.axis_index("expert")]).astype(jnp.int32)
    others = range(1, groups)
    fence = lax.optimization_barrier

    packed, rows = prepare(
        up_weight,
        down_weight,
        grad_out,
        expert_ids,
        gate_weights,
        engram_gate,
        memory_owner,
        memory_slot,
    )
    orders = arrivals(planes)
    came = {}
    zero = (0,) * planes

    def along(step, line):
        even = over_even(line[0]) if step < planes - 1 else None
        return swap(line[1], 4), even

    def arrival(number):
        by_plane = [came[order[number][0]][order[number][1]] for order in orders]
        offsets = tuple(order[number][2] for order in orders)
        return pick(by_plane, plane), offsets

    def plus(share, came_in):
        return (share.astype(jnp.float32) + came_in.astype(jnp.float32)).astype(jnp.bfloat16)

    def reduce(step, sums):
        odd, even = partials[planes - step], partials[step]
        if step > 1 and sums[1] is not None:
            odd = plus(odd, sums[1])
        even = over_even(plus(even, sums[0])) if step > 1 else None
        return swap(odd, 4), even

    half = width // ORDERS
    fits = planes > 3 and folded(lookups // ORDERS * part, half, packed.shape)
    shape = packed.shape if fits else (lookups * part, half)


    rows_x = swap(rows, 2)
    got = [over_expert(rows, step) for step in others]
    came[1] = along(1, (packed, packed))
    late, rows_x = fence((packed, rows_x))
    rows_x, got, near = fence((rows_x, got, swap(rows, 1)))
    grads = [rows] + got
    far = [over_expert(rows_x, step) for step in others]
    near = [near, swap(rows_x, 1)]
    if planes > 2:
        came[2] = along(2, came[1])
        got, far = fence((got, far))
        near, came[2] = fence((near, came[2]))
    blocks = [rows, rows_x, *near, *got, *far]
    for block in got + far:
        blocks += [swap(block[: tok // 2], 1), swap(block[tok // 2 :], 1)]
    partials = table_sums(blocks, place, lookups, part, range(planes), shape)
    for step in range(3, planes - 1 if fits else planes):
        came[step] = along(step, came[step - 1])
    if fits:
        ends = jnp.logical_or(plane == 0, plane == planes - 1)
        met = swap(jnp.where(ends, partials[planes - 1], came[planes - 2][1]), 4)
        came[planes - 1] = (met, None)

    value, where = arrival(0)
    pair = jnp.stack([late, value])
    pair_x = swap(pair, 2)
    later, far = fence((saved_input, far))
    inputs = [over_expert(later, step) for step in others]

    pieces = [(pair, ((zero, 0), (where, 0)))]
    passed, passed_at = pair_x, ((zero, 2), (where, 2))
    todo, near, near_at = pieces[:1], [], []
    sums = ()

    def across(entries):
        return [
            (swap(array, 1), tuple((offsets, flip + 1) for offsets, flip in at))
            for array, at in entries
        ]

    for number in range(2, planes):
        value, where = arrival(number - 1)
        if number == 2:
            partials, value, passed = fence((partials, value, passed))
        else:
            value, passed, inputs = fence((value, passed, inputs))
        pieces += [(passed, passed_at)] + list(zip(near, near_at))
        todo += [(passed, passed_at)]
        moved = across(todo)
        near, near_at = [array for array, _ in moved], [at for _, at in moved]
        passed, passed_at = swap(value, 2), ((where, 2),)
        pieces += [(value, ((where, 0),))]
        todo = [(value, ((where, 0),))]
        if number + 1 == planes:
            moved = across(todo)
            near, near_at = near + [moved[0][0]], near_at + [moved[0][1]]
            todo = []
    pieces += list(zip(near, near_at)) + across(todo)
    inputs = [saved_input] + inputs
    last = (passed_at[0][0], 2)
    hidden = hidden_layers(grads, inputs, pieces, last, place)

    if fits:
        sums = met, None
    for step in range(2 if fits else 1, planes - 1):
        sums = reduce(step, sums)
    sums, hidden, passed = fence((sums, hidden, passed))
    first, second = passed, swap(passed, 1)

    def results(some, begin, dtype):
        return expert_results(
            [grads[g] for g in some],
            [inputs[g] for g in some],
            hidden,
            first,
            second,
            last,
            place,
            lookups,
            top,
            begin * tok,
            dtype,
        )

    if groups > 1:
        rest = results(others, 1, jnp.bfloat16)
        rest, sums = fence((rest, sums))
    if planes > 1:
        sums = reduce(planes - 1, sums)
    returned = [over_expert(rest[(k - 1) * tok : k * tok], groups - k) for k in others]
    total = results([0], 0, jnp.float32)
    for value in returned:
        total = total + value.astype(jnp.float32)
    sums = [partials[0]] + [came_in for came_in in sums[::-1] if came_in is not None]
    table = table_total(sums, lookups * part, half)
    return total.astype(jnp.bfloat16), table.reshape(lookups, part, width // ORDERS)


def solution(mesh):
    return jax.shard_map(
        per_device,
        mesh=mesh,
        in_specs=(
            P(("dp", "expert"), None),
            P(("dp", "expert"), None),
            P(("dp", "expert"), None),
            P(("dp", "expert"), None),
            P("expert", "dp", None),
            P("expert", "dp", None),
            P(("dp", "expert"), None),
            P(("dp", "expert"), None),
            P(("dp", "expert"), None),
        ),
        out_specs=(P(("dp", "expert"), None), P(None, ("dp", "expert"), None)),
        check_vma=False,
    )
```

```python
import functools
import math

import jax
import jax.numpy as jnp
from jax import lax
from jax.experimental import pallas as pl
from jax.experimental.pallas import tpu as pltpu
from jax.sharding import PartitionSpec as P

ORDERS = 2
SHARD = 128
LANES = 128


def silu_slope(pre):
    sig = jax.nn.sigmoid(pre)
    return sig * (1.0 + pre * (1.0 - sig))


def swap(value, bit):
    size = lax.axis_size("dp")
    return lax.ppermute(value, "dp", [(i, i ^ bit) for i in range(size)])


def over_expert(value, step):
    size = lax.axis_size("expert")
    return lax.ppermute(value, "expert", [(i, (i + step) % size) for i in range(size)])


def over_even(value):
    planes = lax.axis_size("dp") // 4
    pairs = []
    for z in range(1, planes - 1, 2):
        for i in range(z * 4, z * 4 + 4):
            pairs += [(i, i + 4), (i + 4, i)]
    return lax.ppermute(value, "dp", pairs)


def room(*arrays):
    return sum(math.prod(shape) * size for shape, size in arrays) + (2 << 20)


def pick(by_plane, plane):
    value = by_plane[-1]
    for z in range(len(by_plane) - 2, -1, -1):
        if by_plane[z] is not by_plane[z + 1]:
            value = jnp.where(plane <= z, by_plane[z], value)
    return value


def arrivals(planes):
    orders = []
    for z in range(planes):
        order = []
        for step in range(1, planes):
            for kind in (0, 1):
                offset = step if (z + kind) % 2 == 0 else -step
                if 0 <= z + offset < planes:
                    order.append((step, kind, offset))
        orders.append(order)
    return orders


def prepare_kernel(up_ref, down_ref, grad_ref, *refs):
    ids_ref, weights_ref, gate_ref, owner_ref, slot_ref, packed_ref, rows_ref, meta_ref = refs
    blocks, rows, cols = packed_ref.shape[1] // 2, packed_ref.shape[2], packed_ref.shape[3]
    for e in range(packed_ref.shape[0]):
        for b in range(blocks):
            packed_ref[e, b] = up_ref[e, b * rows : (b + 1) * rows, :]
            packed_ref[e, blocks + b] = down_ref[e, :, b * cols : (b + 1) * cols]
    tok, width = grad_ref.shape
    rows_ref[:, pl.ds(0, width)] = grad_ref[...]
    weights = weights_ref[...]
    high = weights.astype(jnp.bfloat16).astype(jnp.float32)
    meta_ref[...] = jnp.zeros_like(meta_ref)
    at = 0
    for value in (
        owner_ref[...].astype(jnp.float32),
        slot_ref[...].astype(jnp.float32),
        gate_ref[...],
        ids_ref[...].astype(jnp.float32),
        high,
        weights - high,
    ):
        meta_ref[pl.ds(at, value.shape[0]), :] = value
        at += value.shape[0]
    rows_ref[:, pl.ds(width, LANES)] = meta_ref[...].T.astype(jnp.bfloat16)


def prepare(up, down, grad_out, expert_ids, gate_weights, engram_gate, owner, slot):
    experts, _, hid = up.shape
    rows, width = down.shape[1:]
    tok = grad_out.shape[0]
    return pl.pallas_call(
        prepare_kernel,
        out_shape=(
            jax.ShapeDtypeStruct((experts, 2 * (width // hid), rows, hid), up.dtype),
            jax.ShapeDtypeStruct((tok, width + LANES), grad_out.dtype),
        ),
        scratch_shapes=[pltpu.VMEM((LANES, tok), jnp.float32)],
    )(up, down, grad_out, expert_ids.T, gate_weights.T, engram_gate.T, owner.T, slot.T)


def unstacked(refs):
    dims = min(ref.ndim for ref in refs)
    blocks = []
    for ref in refs:
        blocks += [ref] if ref.ndim == dims else [ref.at[i] for i in range(ref.shape[0])]
    return blocks


def folded(rows, width, shape):
    _, count, deep, wide = shape
    return (
        shape[0] == ORDERS
        and width % (wide // 2) == 0
        and rows % (2 * deep) == 0
        and (width // (wide // 2)) * (rows // (2 * deep)) == count
    )


def folds(rows, width, shape):
    _, _, deep, wide = shape
    for b in range(width // (wide // 2)):
        for h in range(rows // (2 * deep)):
            for u in range(2):
                yield (
                    b * (rows // (2 * deep)) + h,
                    u * (wide // 2),
                    (2 * h + u) * deep,
                    b * (wide // 2),
                )


def table_kernel(lookups, part, planes, offsets, place_ref, *refs):
    count = len(offsets)
    blocks = unstacked(refs[: -count - 3])
    outs, tokens, routing, sem = refs[-count - 3 : -3], refs[-3], refs[-2], refs[-1]
    width = tokens.shape[1]
    half = width // ORDERS
    heads = lookups // ORDERS
    firsts, copies, at = [], [], 0
    for b, block in enumerate(blocks):
        span = pl.ds(at, block.shape[0])
        firsts.append(
            pltpu.make_async_copy(
                block.at[:, pl.ds(width, LANES)], routing.at[span], sem.at[0, b]
            )
        )
        copies.append(
            pltpu.make_async_copy(block.at[:, pl.ds(0, width)], tokens.at[span], sem.at[1, b])
        )
        at += block.shape[0]
    for copy in firsts + copies:
        copy.start()
    for copy in firsts:
        copy.wait()
    metas = [
        routing[pl.ds(first, LANES), :].astype(jnp.float32).T for first in range(0, at, LANES)
    ]
    meta = jnp.concatenate([m[: 3 * lookups] for m in metas], axis=1)
    key = meta[:lookups] * SHARD + meta[lookups : 2 * lookups]
    gate = meta[2 * lookups :]
    me, expert = place_ref[0], place_ref[1]
    plane = me // 4
    row = lax.broadcasted_iota(jnp.int32, (part, at), 0)
    size = heads * part
    hits = []
    for o in range(ORDERS):
        for offset in offsets:
            to = lax.rem(jnp.where(plane % 2 == 0, plane + offset, plane + planes - offset), planes)
            to = to * 4 + me % 4
            rows = (row + (to * SHARD + expert * part)).astype(jnp.float32)
            for j in range(o * heads, (o + 1) * heads):
                hit = jnp.where(rows == key[j : j + 1], gate[j : j + 1], 0.0)
                hits.append(hit.astype(jnp.bfloat16))
    for copy in copies:
        copy.wait()
    for o in range(ORDERS):
        mine = hits[o * heads * count : (o + 1) * heads * count]
        sums = jnp.dot(
            jnp.concatenate(mine, axis=0),
            tokens[:, pl.ds(o * half, half)],
            preferred_element_type=jnp.float32,
        )
        for number, out in enumerate(outs):
            value = sums[number * size : (number + 1) * size].astype(out.dtype)
            if len(out.shape) == 2:
                out[pl.ds(o * size, size), :] = value
                continue
            deep, wide = out.shape[2], out.shape[3] // 2
            for block, lane, at, column in folds(size, half, out.shape):
                out[o, block, :, pl.ds(lane, wide)] = value[at : at + deep, column : column + wide]


def table_sums(blocks, place, lookups, part, offsets, shape):
    total = blocks[0].shape[1]
    planes = lax.axis_size("dp") // 4
    rows, half = lookups * part, (total - LANES) // ORDERS
    count = sum(block.shape[0] for block in blocks)
    return pl.pallas_call(
        functools.partial(table_kernel, lookups, part, planes, tuple(offsets)),
        out_shape=tuple(
            jax.ShapeDtypeStruct(shape, jnp.bfloat16 if offset else jnp.float32)
            for offset in offsets
        ),
        in_specs=[pl.BlockSpec(memory_space=pltpu.SMEM)]
        + [pl.BlockSpec(memory_space=pl.ANY)] * len(blocks),
        scratch_shapes=[
            pltpu.VMEM((count, total - LANES), jnp.bfloat16),
            pltpu.VMEM((count, LANES), jnp.bfloat16),
            pltpu.SemaphoreType.DMA((2, len(blocks))),
        ],
        compiler_params=pltpu.CompilerParams(
            vmem_limit_bytes=room(
                ((count, total), 2), ((len(offsets) + 1, rows, half), 4), ((len(offsets), rows, count), 2)
            )
        ),
        cost_estimate=pl.CostEstimate(
            flops=2 * len(offsets) * rows * count * half,
            bytes_accessed=1 << 12,
            transcendentals=0,
        ),
    )(place, *blocks)


def table_total_kernel(*refs):
    values, out = refs[:-1], refs[-1]
    if len(values[0].shape) == 2:
        out[...] = sum(value[...].astype(jnp.float32) for value in values)
        return
    size, width = out.shape[0] // ORDERS, out.shape[1]
    deep, wide = values[0].shape[2], values[0].shape[3] // 2
    for o in range(ORDERS):
        for block, lane, at, column in folds(size, width, values[0].shape):
            out[pl.ds(o * size + at, deep), pl.ds(column, wide)] = sum(
                value[o, block, :, pl.ds(lane, wide)].astype(jnp.float32) for value in values
            )


def table_total(values, rows, width):
    return pl.pallas_call(
        table_total_kernel,
        out_shape=jax.ShapeDtypeStruct((rows, width), jnp.float32),
        compiler_params=pltpu.CompilerParams(
            vmem_limit_bytes=room(((len(values) + 1, rows, width), 4))
        ),
    )(*values)


def located(where, place_ref, planes):
    offsets, flip = where
    me = place_ref[0]
    at = jnp.bitwise_xor(me, flip)
    for z, offset in enumerate(offsets):
        if offset:
            at = at + jnp.where(me // 4 == z, 4 * offset, 0)
    return at


def token_copies(tokens, targets, sem):
    groups = len(tokens) // 2
    tok = tokens[0].shape[0]
    copies = []
    for number, token in enumerate(tokens):
        target, g = targets[number // groups], number % groups
        copies.append(
            pltpu.make_async_copy(
                token, target.at[pl.ds(g * tok, tok)], sem.at[number // groups, g]
            )
        )
    return copies


def row_chunk(groups, tok):
    return 2 * tok if groups % 2 == 0 else tok


def hidden_kernel(where, last, groups, planes, *refs):
    place_ref, tokens, refs = refs[0], refs[1 : 1 + 2 * groups], refs[1 + 2 * groups :]
    pieces, refs = unstacked(refs[:-9]), refs[-9:]
    turned_ref, pre_ref, back_ref, grad, inp, up, down, token_sem, piece_sem = refs
    experts, blocks, size, rows, hid = down.shape
    copies = token_copies(tokens, (grad, inp), token_sem)
    for number, piece in enumerate(pieces):
        at = located(where[number], place_ref, planes)
        copies.append(
            pltpu.make_async_copy(
                piece.at[:, pl.ds(0, blocks)],
                up.at[:, pl.ds(at * blocks, blocks)],
                piece_sem.at[0, number],
            )
        )
        copies.append(
            pltpu.make_async_copy(
                piece.at[:, pl.ds(blocks, blocks)], down.at[:, :, at], piece_sem.at[1, number]
            )
        )
    for copy in copies:
        copy.start()
    for copy in copies:
        copy.wait()
    pair = located(last, place_ref, planes) // 2
    up[:, pl.ds(pair * 2 * blocks, 2 * blocks)] = jnp.zeros(
        (experts, 2 * blocks, rows, hid), up.dtype
    )
    tok = tokens[0].shape[0]
    chunk = row_chunk(groups, tok)
    for e in range(experts):
        for b in range(blocks):
            block = up[e, b * size : (b + 1) * size].reshape(size * rows, hid)
            turned_ref[e, :, pl.ds(b * hid, hid)] = block.T
    for start in range(0, groups * tok, chunk):
        span = pl.ds(start, chunk)
        for e in range(experts):
            pre = jnp.zeros((chunk, hid), jnp.float32)
            back = jnp.zeros((chunk, hid), jnp.float32)
            for b in range(blocks):
                cols = pl.ds(b * hid, hid)
                pre += jnp.dot(
                    inp[span, cols],
                    up[e, b * size : (b + 1) * size].reshape(size * rows, hid),
                    preferred_element_type=jnp.float32,
                )
                back += lax.dot_general(
                    grad[span, cols],
                    down[e, b].reshape(size * rows, hid),
                    (((1,), (1,)), ((), ())),
                    preferred_element_type=jnp.float32,
                )
            pre_ref[span, pl.ds(e * hid, hid)] = pre
            back_ref[span, pl.ds(e * hid, hid)] = back


def slab_of(blocks, rows):
    held = 2 * blocks * rows
    return held, -(-(LANES - math.gcd(held, LANES) + held) // LANES) * LANES


def result_kernel(last, begin, groups, planes, lookups, top, *refs):
    place_ref, tokens, refs = refs[0], refs[1 : 1 + 2 * groups], refs[1 + 2 * groups :]
    turned_ref, first_ref, second_ref, pre_ref, back_ref, out_ref, *refs = refs
    grad, part, up, down, back_part, token_sem, piece_sem = refs
    count, width = out_ref.shape
    tok = count // groups
    experts, blocks, per, rows, hid = down.shape
    expert = place_ref[1]
    pair = located(last, place_ref, planes) // 2
    held, slab = slab_of(blocks, rows)
    base = pl.multiple_of(pair * held // LANES * LANES, LANES)
    skip = lax.rem(pair * held, LANES)

    up[...] = jnp.zeros_like(up)
    copies = token_copies(
        list(tokens[:groups]) + [token.at[:, pl.ds(base, slab)] for token in tokens[groups:]],
        (grad, part),
        token_sem,
    )
    for number, piece in enumerate((first_ref, second_ref)):
        at = located((last[0], last[1] + number), place_ref, planes)
        copies.append(
            pltpu.make_async_copy(
                piece.at[:, pl.ds(0, blocks)],
                up.at[:, pl.ds(skip // rows + lax.rem(at, 2) * blocks, blocks)],
                piece_sem.at[0, number],
            )
        )
        copies.append(
            pltpu.make_async_copy(
                piece.at[:, pl.ds(blocks, blocks)],
                down.at[:, :, lax.rem(at, per)],
                piece_sem.at[1, number],
            )
        )
    mine = pl.ds(begin, count)
    copies.append(pltpu.make_async_copy(back_ref.at[mine], back_part, piece_sem.at[1, 2]))
    for copy in copies:
        copy.start()
    for copy in copies:
        copy.wait()

    hid_slab = pl.multiple_of(pair * 2 // per * LANES, LANES)
    hid_skip = lax.rem(pair * 2, per) * rows
    chunk = row_chunk(groups, tok)
    at = 3 * lookups
    lane = lax.broadcasted_iota(jnp.int32, (chunk, slab), 1)
    lane = jnp.logical_and(lane >= skip, lane < skip + held)
    hid_lane = lax.broadcasted_iota(jnp.int32, (chunk, LANES), 1)
    hid_lane = jnp.logical_and(hid_lane >= hid_skip, hid_lane < hid_skip + 2 * rows)
    for start in range(0, groups * tok, chunk):
        span = pl.ds(start, chunk)
        meta = grad[span, pl.ds(width, LANES)].astype(jnp.float32)
        mine = jnp.where(lane, part[span, :].astype(jnp.float32), 0.0).astype(jnp.bfloat16)
        slopes = []
        for e in range(experts):
            units = pl.ds(e * hid, hid)
            pre = pre_ref[pl.ds(begin + start, chunk), units] + jnp.dot(
                mine, up[e].reshape(slab, hid), preferred_element_type=jnp.float32
            )
            late = jnp.zeros((chunk, LANES), jnp.float32)
            for b in range(blocks):
                late += lax.dot_general(
                    grad[span, pl.ds(b * hid, hid)],
                    down[e, b].reshape(LANES, hid),
                    (((1,), (1,)), ((), ())),
                    preferred_element_type=jnp.float32,
                )
            lanes = pl.ds(pl.multiple_of(e * hid + hid_slab, LANES), LANES)
            back_part[span, lanes] = jnp.where(hid_lane, late, back_part[span, lanes])
            weight = jnp.zeros((chunk, 1), jnp.float32)
            number = (expert * experts + e).astype(jnp.float32)
            for k in range(top):
                value = meta[:, at + top + k : at + top + k + 1]
                value += meta[:, at + 2 * top + k : at + 2 * top + k + 1]
                weight += jnp.where(meta[:, at + k : at + k + 1] == number, value, 0.0)
            slope = back_part[span, units] * silu_slope(pre) * weight
            slopes.append(slope.astype(jnp.bfloat16))
        for b in range(blocks):
            cols = pl.ds(b * hid, hid)
            total = jnp.zeros((chunk, hid), jnp.float32)
            for e in range(experts):
                total += jnp.dot(
                    slopes[e], turned_ref[e, :, cols], preferred_element_type=jnp.float32
                )
            out_ref[span, cols] = total.astype(out_ref.dtype)
        late = jnp.zeros((chunk, slab), jnp.float32)
        for e in range(experts):
            late += lax.dot_general(
                slopes[e],
                up[e].reshape(slab, hid),
                (((1,), (1,)), ((), ())),
                preferred_element_type=jnp.float32,
            )
        cols = pl.ds(base, slab)
        known = out_ref[span, cols].astype(jnp.float32)
        out_ref[span, cols] = (known + late).astype(out_ref.dtype)


def hidden_layers(grads, inputs, pieces, last, place):
    groups = len(grads)
    tok, width = inputs[0].shape
    experts, blocks2, rows, hid = pieces[0][0].shape[-4:]
    blocks = blocks2 // 2
    dp = lax.axis_size("dp")
    where = tuple(entry for _, entries in pieces for entry in entries)
    any_space, vmem = pl.BlockSpec(memory_space=pl.ANY), pl.BlockSpec(memory_space=pltpu.VMEM)
    return pl.pallas_call(
        functools.partial(hidden_kernel, where, last, groups, dp // 4),
        out_shape=(
            jax.ShapeDtypeStruct((experts, hid, width), jnp.bfloat16),
            jax.ShapeDtypeStruct((groups * tok, experts * hid), jnp.float32),
            jax.ShapeDtypeStruct((groups * tok, experts * hid), jnp.float32),
        ),
        in_specs=[pl.BlockSpec(memory_space=pltpu.SMEM)]
        + [any_space] * (2 * groups + len(pieces)),
        out_specs=(vmem, vmem, vmem),
        scratch_shapes=[
            pltpu.VMEM((groups * tok, width + LANES), jnp.bfloat16),
            pltpu.VMEM((groups * tok, width), jnp.bfloat16),
            pltpu.VMEM((experts, dp * blocks, rows, hid), jnp.bfloat16),
            pltpu.VMEM((experts, blocks, dp, rows, hid), jnp.bfloat16),
            pltpu.SemaphoreType.DMA((2, groups)),
            pltpu.SemaphoreType.DMA((2, len(where))),
        ],
        compiler_params=pltpu.CompilerParams(
            vmem_limit_bytes=room(
                ((groups * tok, 2 * width + LANES), 2),
                ((3, experts, hid, width), 2),
                ((2, groups * tok, experts * hid), 4),
            )
        ),
        cost_estimate=pl.CostEstimate(
            flops=4 * groups * tok * width * hid * experts,
            bytes_accessed=6 * experts * width * hid + 8 * groups * tok * width,
            transcendentals=0,
        ),
    )(place, *grads, *inputs, *[piece[0] for piece in pieces])


def expert_results(grads, inputs, hidden, first, second, last, place, lookups, top, begin, dtype):
    groups = len(grads)
    tok, width = inputs[0].shape
    experts, blocks2, rows, hid = first.shape
    blocks = blocks2 // 2
    dp = lax.axis_size("dp")
    turned, pre, back = hidden
    slab = slab_of(blocks, rows)[1]
    any_space, vmem = pl.BlockSpec(memory_space=pl.ANY), pl.BlockSpec(memory_space=pltpu.VMEM)
    return pl.pallas_call(
        functools.partial(result_kernel, last, begin, groups, dp // 4, lookups, top),
        out_shape=jax.ShapeDtypeStruct((groups * tok, width), dtype),
        in_specs=[pl.BlockSpec(memory_space=pltpu.SMEM)]
        + [any_space] * (2 * groups)
        + [vmem, any_space, any_space, vmem, any_space],
        out_specs=vmem,
        scratch_shapes=[
            pltpu.VMEM((groups * tok, width + LANES), jnp.bfloat16),
            pltpu.VMEM((groups * tok, slab), jnp.bfloat16),
            pltpu.VMEM((experts, slab // rows, rows, hid), jnp.bfloat16),
            pltpu.VMEM((experts, blocks, LANES // rows, rows, hid), jnp.bfloat16),
            pltpu.VMEM((groups * tok, back.shape[1]), jnp.float32),
            pltpu.SemaphoreType.DMA((2, groups)),
            pltpu.SemaphoreType.DMA((2, 3)),
        ],
        compiler_params=pltpu.CompilerParams(
            vmem_limit_bytes=room(
                ((groups * tok, width + LANES + slab), 2),
                ((experts, hid, width + slab), 2),
                ((experts, LANES, width), 2),
                ((2, groups * tok, experts * hid), 4),
                ((groups * tok, width), 4),
            )
        ),
        cost_estimate=pl.CostEstimate(
            flops=2 * groups * tok * width * hid * experts,
            bytes_accessed=2 * experts * width * hid + 12 * groups * tok * width,
            transcendentals=groups * tok * hid * experts,
        ),
    )(place, *grads, *inputs, turned, first, second, pre, back)


def per_device(
    grad_out,
    saved_input,
    expert_ids,
    gate_weights,
    up_weight,
    down_weight,
    engram_gate,
    memory_owner,
    memory_slot,
):
    tok, width = grad_out.shape
    lookups, top = engram_gate.shape[1], expert_ids.shape[1]
    groups = lax.axis_size("expert")
    planes = lax.axis_size("dp") // 4
    part = SHARD // groups
    me = lax.axis_index("dp")
    plane = me // 4
    place = jnp.stack([me, lax.axis_index("expert")]).astype(jnp.int32)
    others = range(1, groups)
    fence = lax.optimization_barrier

    packed, rows = prepare(
        up_weight,
        down_weight,
        grad_out,
        expert_ids,
        gate_weights,
        engram_gate,
        memory_owner,
        memory_slot,
    )
    orders = arrivals(planes)
    came = {}
    zero = (0,) * planes

    def along(step, line):
        even = over_even(line[0]) if step < planes - 1 else None
        return swap(line[1], 4), even

    def arrival(number):
        by_plane = [came[order[number][0]][order[number][1]] for order in orders]
        offsets = tuple(order[number][2] for order in orders)
        return pick(by_plane, plane), offsets

    def plus(share, came_in):
        return (share.astype(jnp.float32) + came_in.astype(jnp.float32)).astype(jnp.bfloat16)

    def reduce(step, sums):
        odd, even = partials[planes - step], partials[step]
        if step > 1 and sums[1] is not None:
            odd = plus(odd, sums[1])
        even = over_even(plus(even, sums[0])) if step > 1 else None
        return swap(odd, 4), even

    half = width // ORDERS
    fits = planes > 3 and folded(lookups // ORDERS * part, half, packed.shape)
    shape = packed.shape if fits else (lookups * part, half)


    rows_x = swap(rows, 2)
    got = [over_expert(rows, step) for step in others]
    came[1] = along(1, (packed, packed))
    late, rows_x = fence((packed, rows_x))
    rows_x, got, near = fence((rows_x, got, swap(rows, 1)))
    grads = [rows] + got
    far = [over_expert(rows_x, step) for step in others]
    near = [near, swap(rows_x, 1)]
    if planes > 2:
        came[2] = along(2, came[1])
        got, far = fence((got, far))
        near, came[2] = fence((near, came[2]))
    blocks = [rows, rows_x, *near, *got, *far]
    for block in got + far:
        blocks += [swap(block[: tok // 2], 1), swap(block[tok // 2 :], 1)]
    partials = table_sums(blocks, place, lookups, part, range(planes), shape)
    for step in range(3, planes - 1 if fits else planes):
        came[step] = along(step, came[step - 1])
    if fits:
        ends = jnp.logical_or(plane == 0, plane == planes - 1)
        met = swap(jnp.where(ends, partials[planes - 1], came[planes - 2][1]), 4)
        came[planes - 1] = (met, None)

    value, where = arrival(0)
    pair = jnp.stack([late, value])
    pair_x = swap(pair, 2)
    later, far = fence((saved_input, far))
    inputs = [over_expert(later, step) for step in others]

    pieces = [(pair, ((zero, 0), (where, 0)))]
    passed, passed_at = pair_x, ((zero, 2), (where, 2))
    todo, near, near_at = pieces[:1], [], []
    sums = ()

    def across(entries):
        return [
            (swap(array, 1), tuple((offsets, flip + 1) for offsets, flip in at))
            for array, at in entries
        ]

    for number in range(2, planes):
        value, where = arrival(number - 1)
        if number == 2:
            partials, value, passed = fence((partials, value, passed))
        else:
            value, passed, inputs = fence((value, passed, inputs))
        pieces += [(passed, passed_at)] + list(zip(near, near_at))
        todo += [(passed, passed_at)]
        moved = across(todo)
        near, near_at = [array for array, _ in moved], [at for _, at in moved]
        passed, passed_at = swap(value, 2), ((where, 2),)
        pieces += [(value, ((where, 0),))]
        todo = [(value, ((where, 0),))]
        if number + 1 == planes:
            moved = across(todo)
            near, near_at = near + [moved[0][0]], near_at + [moved[0][1]]
            todo = []
    pieces += list(zip(near, near_at)) + across(todo)
    inputs = [saved_input] + inputs
    last = (passed_at[0][0], 2)
    hidden = hidden_layers(grads, inputs, pieces, last, place)

    if fits:
        sums = met, None
    for step in range(2 if fits else 1, planes - 1):
        sums = reduce(step, sums)
    sums, hidden, passed = fence((sums, hidden, passed))
    first, second = passed, swap(passed, 1)

    def results(some, begin, dtype):
        return expert_results(
            [grads[g] for g in some],
            [inputs[g] for g in some],
            hidden,
            first,
            second,
            last,
            place,
            lookups,
            top,
            begin * tok,
            dtype,
        )

    if groups > 1:
        rest = results(others, 1, jnp.bfloat16)
        rest, sums = fence((rest, sums))
    if planes > 1:
        sums = reduce(planes - 1, sums)
    returned = [over_expert(rest[(k - 1) * tok : k * tok], groups - k) for k in others]
    total = results([0], 0, jnp.float32)
    for value in returned:
        total = total + value.astype(jnp.float32)
    sums = [partials[0]] + [came_in for came_in in sums[::-1] if came_in is not None]
    table = table_total(sums, lookups * part, half)
    return total.astype(jnp.bfloat16), table.reshape(lookups, part, width // ORDERS)


def solution(mesh):
    return jax.shard_map(
        per_device,
        mesh=mesh,
        in_specs=(
            P(("dp", "expert"), None),
            P(("dp", "expert"), None),
            P(("dp", "expert"), None),
            P(("dp", "expert"), None),
            P("expert", "dp", None),
            P("expert", "dp", None),
            P(("dp", "expert"), None),
            P(("dp", "expert"), None),
            P(("dp", "expert"), None),
        ),
        out_specs=(P(("dp", "expert"), None), P(None, ("dp", "expert"), None)),
        check_vma=False,
    )
```

```python
import functools
import math

import jax
import jax.numpy as jnp
from jax import lax
from jax.experimental import pallas as pl
from jax.experimental.pallas import tpu as pltpu
from jax.sharding import PartitionSpec as P

ORDERS = 2
SHARD = 128
LANES = 128


def silu_slope(pre):
    sig = jax.nn.sigmoid(pre)
    return sig * (1.0 + pre * (1.0 - sig))


def swap(value, bit):
    size = lax.axis_size("dp")
    return lax.ppermute(value, "dp", [(i, i ^ bit) for i in range(size)])


def over_expert(value, step):
    size = lax.axis_size("expert")
    return lax.ppermute(value, "expert", [(i, (i + step) % size) for i in range(size)])


def over_even(value):
    planes = lax.axis_size("dp") // 4
    pairs = []
    for z in range(1, planes - 1, 2):
        for i in range(z * 4, z * 4 + 4):
            pairs += [(i, i + 4), (i + 4, i)]
    return lax.ppermute(value, "dp", pairs)


def room(*arrays):
    return sum(math.prod(shape) * size for shape, size in arrays) + (2 << 20)


def pick(by_plane, plane):
    value = by_plane[-1]
    for z in range(len(by_plane) - 2, -1, -1):
        if by_plane[z] is not by_plane[z + 1]:
            value = jnp.where(plane <= z, by_plane[z], value)
    return value


def arrivals(planes):
    orders = []
    for z in range(planes):
        order = []
        for step in range(1, planes):
            for kind in (0, 1):
                offset = step if (z + kind) % 2 == 0 else -step
                if 0 <= z + offset < planes:
                    order.append((step, kind, offset))
        orders.append(order)
    return orders


def prepare_kernel(up_ref, down_ref, grad_ref, *refs):
    ids_ref, weights_ref, gate_ref, owner_ref, slot_ref, packed_ref, rows_ref, meta_ref, sem = refs
    blocks, rows, cols = packed_ref.shape[1] // 2, packed_ref.shape[2], packed_ref.shape[3]
    tok, width = grad_ref.shape
    copies = [pltpu.make_async_copy(grad_ref, rows_ref.at[:, pl.ds(0, width)], sem.at[0])]
    for e in range(packed_ref.shape[0]):
        for b in range(blocks):
            for source, at in (
                (up_ref.at[e, pl.ds(b * rows, rows)], b),
                (down_ref.at[e, :, pl.ds(b * cols, cols)], blocks + b),
            ):
                copies.append(
                    pltpu.make_async_copy(source, packed_ref.at[e, at], sem.at[len(copies)])
                )
    for copy in copies:
        copy.start()
    weights = weights_ref[...]
    high = weights.astype(jnp.bfloat16).astype(jnp.float32)
    meta_ref[...] = jnp.zeros_like(meta_ref)
    at = 0
    for value in (
        owner_ref[...].astype(jnp.float32),
        slot_ref[...].astype(jnp.float32),
        gate_ref[...],
        ids_ref[...].astype(jnp.float32),
        high,
        weights - high,
    ):
        meta_ref[pl.ds(at, value.shape[0]), :] = value
        at += value.shape[0]
    rows_ref[:, pl.ds(width, LANES)] = meta_ref[...].T.astype(jnp.bfloat16)
    for copy in copies:
        copy.wait()


def prepare(up, down, grad_out, expert_ids, gate_weights, engram_gate, owner, slot):
    experts, _, hid = up.shape
    rows, width = down.shape[1:]
    tok = grad_out.shape[0]
    return pl.pallas_call(
        prepare_kernel,
        out_shape=(
            jax.ShapeDtypeStruct((experts, 2 * (width // hid), rows, hid), up.dtype),
            jax.ShapeDtypeStruct((tok, width + LANES), grad_out.dtype),
        ),
        in_specs=[pl.BlockSpec(memory_space=pl.ANY)] * 3
        + [pl.BlockSpec(memory_space=pltpu.VMEM)] * 5,
        scratch_shapes=[
            pltpu.VMEM((LANES, tok), jnp.float32),
            pltpu.SemaphoreType.DMA((1 + 2 * experts * (width // hid),)),
        ],
    )(up, down, grad_out, expert_ids.T, gate_weights.T, engram_gate.T, owner.T, slot.T)


def unstacked(refs):
    dims = min(ref.ndim for ref in refs)
    blocks = []
    for ref in refs:
        blocks += [ref] if ref.ndim == dims else [ref.at[i] for i in range(ref.shape[0])]
    return blocks


def folded(rows, width, shape):
    _, count, deep, wide = shape
    return (
        shape[0] == ORDERS
        and width % (wide // 2) == 0
        and rows % (2 * deep) == 0
        and (width // (wide // 2)) * (rows // (2 * deep)) == count
    )


def folds(rows, width, shape):
    _, _, deep, wide = shape
    for b in range(width // (wide // 2)):
        for h in range(rows // (2 * deep)):
            for u in range(2):
                yield (
                    b * (rows // (2 * deep)) + h,
                    u * (wide // 2),
                    (2 * h + u) * deep,
                    b * (wide // 2),
                )


def table_kernel(lookups, part, planes, offsets, place_ref, *refs):
    count = len(offsets)
    blocks = unstacked(refs[: -count - 3])
    outs, tokens, routing, sem = refs[-count - 3 : -3], refs[-3], refs[-2], refs[-1]
    width = tokens.shape[1]
    half = width // ORDERS
    heads = lookups // ORDERS
    firsts, copies, at = [], [], 0
    for b, block in enumerate(blocks):
        span = pl.ds(at, block.shape[0])
        firsts.append(
            pltpu.make_async_copy(
                block.at[:, pl.ds(width, LANES)], routing.at[span], sem.at[0, b]
            )
        )
        copies.append(
            pltpu.make_async_copy(block.at[:, pl.ds(0, width)], tokens.at[span], sem.at[1, b])
        )
        at += block.shape[0]
    for copy in firsts + copies:
        copy.start()
    for copy in firsts:
        copy.wait()
    metas = [
        routing[pl.ds(first, LANES), :].astype(jnp.float32).T for first in range(0, at, LANES)
    ]
    meta = jnp.concatenate([m[: 3 * lookups] for m in metas], axis=1)
    key = meta[:lookups] * SHARD + meta[lookups : 2 * lookups]
    gate = meta[2 * lookups :]
    me, expert = place_ref[0], place_ref[1]
    plane = me // 4
    row = lax.broadcasted_iota(jnp.int32, (part, at), 0)
    size = heads * part
    hits = []
    for o in range(ORDERS):
        for offset in offsets:
            to = lax.rem(jnp.where(plane % 2 == 0, plane + offset, plane + planes - offset), planes)
            to = to * 4 + me % 4
            rows = (row + (to * SHARD + expert * part)).astype(jnp.float32)
            for j in range(o * heads, (o + 1) * heads):
                hit = jnp.where(rows == key[j : j + 1], gate[j : j + 1], 0.0)
                hits.append(hit.astype(jnp.bfloat16))
    for copy in copies:
        copy.wait()
    for o in range(ORDERS):
        mine = hits[o * heads * count : (o + 1) * heads * count]
        sums = jnp.dot(
            jnp.concatenate(mine, axis=0),
            tokens[:, pl.ds(o * half, half)],
            preferred_element_type=jnp.float32,
        )
        for number, out in enumerate(outs):
            value = sums[number * size : (number + 1) * size].astype(out.dtype)
            if len(out.shape) == 2:
                out[pl.ds(o * size, size), :] = value
                continue
            deep, wide = out.shape[2], out.shape[3] // 2
            for block, lane, at, column in folds(size, half, out.shape):
                out[o, block, :, pl.ds(lane, wide)] = value[at : at + deep, column : column + wide]


def table_sums(blocks, place, lookups, part, offsets, shape):
    total = blocks[0].shape[1]
    planes = lax.axis_size("dp") // 4
    rows, half = lookups * part, (total - LANES) // ORDERS
    count = sum(block.shape[0] for block in blocks)
    return pl.pallas_call(
        functools.partial(table_kernel, lookups, part, planes, tuple(offsets)),
        out_shape=tuple(
            jax.ShapeDtypeStruct(shape, jnp.bfloat16 if offset else jnp.float32)
            for offset in offsets
        ),
        in_specs=[pl.BlockSpec(memory_space=pltpu.SMEM)]
        + [pl.BlockSpec(memory_space=pl.ANY)] * len(blocks),
        scratch_shapes=[
            pltpu.VMEM((count, total - LANES), jnp.bfloat16),
            pltpu.VMEM((count, LANES), jnp.bfloat16),
            pltpu.SemaphoreType.DMA((2, len(blocks))),
        ],
        compiler_params=pltpu.CompilerParams(
            vmem_limit_bytes=room(
                ((count, total), 2), ((len(offsets) + 1, rows, half), 4), ((len(offsets), rows, count), 2)
            )
        ),
        cost_estimate=pl.CostEstimate(
            flops=2 * len(offsets) * rows * count * half,
            bytes_accessed=1 << 12,
            transcendentals=0,
        ),
    )(place, *blocks)


def table_total_kernel(*refs):
    values, out = refs[:-1], refs[-1]
    if len(values[0].shape) == 2:
        out[...] = sum(value[...].astype(jnp.float32) for value in values)
        return
    size, width = out.shape[0] // ORDERS, out.shape[1]
    deep, wide = values[0].shape[2], values[0].shape[3] // 2
    for o in range(ORDERS):
        for block, lane, at, column in folds(size, width, values[0].shape):
            out[pl.ds(o * size + at, deep), pl.ds(column, wide)] = sum(
                value[o, block, :, pl.ds(lane, wide)].astype(jnp.float32) for value in values
            )


def table_total(values, rows, width):
    return pl.pallas_call(
        table_total_kernel,
        out_shape=jax.ShapeDtypeStruct((rows, width), jnp.float32),
        compiler_params=pltpu.CompilerParams(
            vmem_limit_bytes=room(((len(values) + 1, rows, width), 4))
        ),
    )(*values)


def located(where, place_ref, planes):
    offsets, flip = where
    me = place_ref[0]
    at = jnp.bitwise_xor(me, flip)
    for z, offset in enumerate(offsets):
        if offset:
            at = at + jnp.where(me // 4 == z, 4 * offset, 0)
    return at


def token_copies(tokens, targets, sem):
    groups = len(tokens) // 2
    tok = tokens[0].shape[0]
    copies = []
    for number, token in enumerate(tokens):
        target, g = targets[number // groups], number % groups
        copies.append(
            pltpu.make_async_copy(
                token, target.at[pl.ds(g * tok, tok)], sem.at[number // groups, g]
            )
        )
    return copies


def row_chunk(groups, tok):
    return 2 * tok if groups % 2 == 0 else tok


def hidden_kernel(where, last, groups, planes, *refs):
    place_ref, tokens, refs = refs[0], refs[1 : 1 + 2 * groups], refs[1 + 2 * groups :]
    pieces, refs = unstacked(refs[:-9]), refs[-9:]
    turned_ref, pre_ref, back_ref, grad, inp, up, down, token_sem, piece_sem = refs
    experts, blocks, size, rows, hid = down.shape
    copies = token_copies(tokens, (grad, inp), token_sem)
    for number, piece in enumerate(pieces):
        at = located(where[number], place_ref, planes)
        copies.append(
            pltpu.make_async_copy(
                piece.at[:, pl.ds(0, blocks)],
                up.at[:, pl.ds(at * blocks, blocks)],
                piece_sem.at[0, number],
            )
        )
        copies.append(
            pltpu.make_async_copy(
                piece.at[:, pl.ds(blocks, blocks)], down.at[:, :, at], piece_sem.at[1, number]
            )
        )
    for copy in copies:
        copy.start()
    for copy in copies:
        copy.wait()
    pair = located(last, place_ref, planes) // 2
    up[:, pl.ds(pair * 2 * blocks, 2 * blocks)] = jnp.zeros(
        (experts, 2 * blocks, rows, hid), up.dtype
    )
    tok = tokens[0].shape[0]
    chunk = row_chunk(groups, tok)
    for e in range(experts):
        for b in range(blocks):
            block = up[e, b * size : (b + 1) * size].reshape(size * rows, hid)
            turned_ref[e, :, pl.ds(b * hid, hid)] = block.T
    for start in range(0, groups * tok, chunk):
        span = pl.ds(start, chunk)
        for e in range(experts):
            pre = jnp.zeros((chunk, hid), jnp.float32)
            back = jnp.zeros((chunk, hid), jnp.float32)
            for b in range(blocks):
                cols = pl.ds(b * hid, hid)
                pre += jnp.dot(
                    inp[span, cols],
                    up[e, b * size : (b + 1) * size].reshape(size * rows, hid),
                    preferred_element_type=jnp.float32,
                )
                back += lax.dot_general(
                    grad[span, cols],
                    down[e, b].reshape(size * rows, hid),
                    (((1,), (1,)), ((), ())),
                    preferred_element_type=jnp.float32,
                )
            pre_ref[span, pl.ds(e * hid, hid)] = pre
            back_ref[span, pl.ds(e * hid, hid)] = back


def slab_of(blocks, rows):
    held = 2 * blocks * rows
    return held, -(-(LANES - math.gcd(held, LANES) + held) // LANES) * LANES


def result_kernel(last, begin, groups, planes, lookups, top, *refs):
    place_ref, tokens, refs = refs[0], refs[1 : 1 + 2 * groups], refs[1 + 2 * groups :]
    turned_ref, first_ref, second_ref, pre_ref, back_ref, out_ref, *refs = refs
    grad, part, up, down, back_part, token_sem, piece_sem = refs
    count, width = out_ref.shape
    tok = count // groups
    experts, blocks, per, rows, hid = down.shape
    expert = place_ref[1]
    pair = located(last, place_ref, planes) // 2
    held, slab = slab_of(blocks, rows)
    base = pl.multiple_of(pair * held // LANES * LANES, LANES)
    skip = lax.rem(pair * held, LANES)

    up[...] = jnp.zeros_like(up)
    copies = token_copies(
        list(tokens[:groups]) + [token.at[:, pl.ds(base, slab)] for token in tokens[groups:]],
        (grad, part),
        token_sem,
    )
    for number, piece in enumerate((first_ref, second_ref)):
        at = located((last[0], last[1] + number), place_ref, planes)
        copies.append(
            pltpu.make_async_copy(
                piece.at[:, pl.ds(0, blocks)],
                up.at[:, pl.ds(skip // rows + lax.rem(at, 2) * blocks, blocks)],
                piece_sem.at[0, number],
            )
        )
        copies.append(
            pltpu.make_async_copy(
                piece.at[:, pl.ds(blocks, blocks)],
                down.at[:, :, lax.rem(at, per)],
                piece_sem.at[1, number],
            )
        )
    mine = pl.ds(begin, count)
    copies.append(pltpu.make_async_copy(back_ref.at[mine], back_part, piece_sem.at[1, 2]))
    for copy in copies:
        copy.start()
    for copy in copies:
        copy.wait()

    hid_slab = pl.multiple_of(pair * 2 // per * LANES, LANES)
    hid_skip = lax.rem(pair * 2, per) * rows
    chunk = row_chunk(groups, tok)
    at = 3 * lookups
    lane = lax.broadcasted_iota(jnp.int32, (chunk, slab), 1)
    lane = jnp.logical_and(lane >= skip, lane < skip + held)
    hid_lane = lax.broadcasted_iota(jnp.int32, (chunk, LANES), 1)
    hid_lane = jnp.logical_and(hid_lane >= hid_skip, hid_lane < hid_skip + 2 * rows)
    for start in range(0, groups * tok, chunk):
        span = pl.ds(start, chunk)
        meta = grad[span, pl.ds(width, LANES)].astype(jnp.float32)
        mine = jnp.where(lane, part[span, :].astype(jnp.float32), 0.0).astype(jnp.bfloat16)
        slopes = []
        for e in range(experts):
            units = pl.ds(e * hid, hid)
            pre = pre_ref[pl.ds(begin + start, chunk), units] + jnp.dot(
                mine, up[e].reshape(slab, hid), preferred_element_type=jnp.float32
            )
            late = jnp.zeros((chunk, LANES), jnp.float32)
            for b in range(blocks):
                late += lax.dot_general(
                    grad[span, pl.ds(b * hid, hid)],
                    down[e, b].reshape(LANES, hid),
                    (((1,), (1,)), ((), ())),
                    preferred_element_type=jnp.float32,
                )
            lanes = pl.ds(pl.multiple_of(e * hid + hid_slab, LANES), LANES)
            back_part[span, lanes] = jnp.where(hid_lane, late, back_part[span, lanes])
            weight = jnp.zeros((chunk, 1), jnp.float32)
            number = (expert * experts + e).astype(jnp.float32)
            for k in range(top):
                value = meta[:, at + top + k : at + top + k + 1]
                value += meta[:, at + 2 * top + k : at + 2 * top + k + 1]
                weight += jnp.where(meta[:, at + k : at + k + 1] == number, value, 0.0)
            slope = back_part[span, units] * silu_slope(pre) * weight
            slopes.append(slope.astype(jnp.bfloat16))
        for b in range(blocks):
            cols = pl.ds(b * hid, hid)
            total = jnp.zeros((chunk, hid), jnp.float32)
            for e in range(experts):
                total += jnp.dot(
                    slopes[e], turned_ref[e, :, cols], preferred_element_type=jnp.float32
                )
            out_ref[span, cols] = total.astype(out_ref.dtype)
        late = jnp.zeros((chunk, slab), jnp.float32)
        for e in range(experts):
            late += lax.dot_general(
                slopes[e],
                up[e].reshape(slab, hid),
                (((1,), (1,)), ((), ())),
                preferred_element_type=jnp.float32,
            )
        cols = pl.ds(base, slab)
        known = out_ref[span, cols].astype(jnp.float32)
        out_ref[span, cols] = (known + late).astype(out_ref.dtype)


def hidden_layers(grads, inputs, pieces, last, place):
    groups = len(grads)
    tok, width = inputs[0].shape
    experts, blocks2, rows, hid = pieces[0][0].shape[-4:]
    blocks = blocks2 // 2
    dp = lax.axis_size("dp")
    where = tuple(entry for _, entries in pieces for entry in entries)
    any_space, vmem = pl.BlockSpec(memory_space=pl.ANY), pl.BlockSpec(memory_space=pltpu.VMEM)
    return pl.pallas_call(
        functools.partial(hidden_kernel, where, last, groups, dp // 4),
        out_shape=(
            jax.ShapeDtypeStruct((experts, hid, width), jnp.bfloat16),
            jax.ShapeDtypeStruct((groups * tok, experts * hid), jnp.float32),
            jax.ShapeDtypeStruct((groups * tok, experts * hid), jnp.float32),
        ),
        in_specs=[pl.BlockSpec(memory_space=pltpu.SMEM)]
        + [any_space] * (2 * groups + len(pieces)),
        out_specs=(vmem, vmem, vmem),
        scratch_shapes=[
            pltpu.VMEM((groups * tok, width + LANES), jnp.bfloat16),
            pltpu.VMEM((groups * tok, width), jnp.bfloat16),
            pltpu.VMEM((experts, dp * blocks, rows, hid), jnp.bfloat16),
            pltpu.VMEM((experts, blocks, dp, rows, hid), jnp.bfloat16),
            pltpu.SemaphoreType.DMA((2, groups)),
            pltpu.SemaphoreType.DMA((2, len(where))),
        ],
        compiler_params=pltpu.CompilerParams(
            vmem_limit_bytes=room(
                ((groups * tok, 2 * width + LANES), 2),
                ((3, experts, hid, width), 2),
                ((2, groups * tok, experts * hid), 4),
            )
        ),
        cost_estimate=pl.CostEstimate(
            flops=4 * groups * tok * width * hid * experts,
            bytes_accessed=6 * experts * width * hid + 8 * groups * tok * width,
            transcendentals=0,
        ),
    )(place, *grads, *inputs, *[piece[0] for piece in pieces])


def expert_results(grads, inputs, hidden, first, second, last, place, lookups, top, begin, dtype):
    groups = len(grads)
    tok, width = inputs[0].shape
    experts, blocks2, rows, hid = first.shape
    blocks = blocks2 // 2
    dp = lax.axis_size("dp")
    turned, pre, back = hidden
    slab = slab_of(blocks, rows)[1]
    any_space, vmem = pl.BlockSpec(memory_space=pl.ANY), pl.BlockSpec(memory_space=pltpu.VMEM)
    return pl.pallas_call(
        functools.partial(result_kernel, last, begin, groups, dp // 4, lookups, top),
        out_shape=jax.ShapeDtypeStruct((groups * tok, width), dtype),
        in_specs=[pl.BlockSpec(memory_space=pltpu.SMEM)]
        + [any_space] * (2 * groups)
        + [vmem, any_space, any_space, vmem, any_space],
        out_specs=vmem,
        scratch_shapes=[
            pltpu.VMEM((groups * tok, width + LANES), jnp.bfloat16),
            pltpu.VMEM((groups * tok, slab), jnp.bfloat16),
            pltpu.VMEM((experts, slab // rows, rows, hid), jnp.bfloat16),
            pltpu.VMEM((experts, blocks, LANES // rows, rows, hid), jnp.bfloat16),
            pltpu.VMEM((groups * tok, back.shape[1]), jnp.float32),
            pltpu.SemaphoreType.DMA((2, groups)),
            pltpu.SemaphoreType.DMA((2, 3)),
        ],
        compiler_params=pltpu.CompilerParams(
            vmem_limit_bytes=room(
                ((groups * tok, width + LANES + slab), 2),
                ((experts, hid, width + slab), 2),
                ((experts, LANES, width), 2),
                ((2, groups * tok, experts * hid), 4),
                ((groups * tok, width), 4),
            )
        ),
        cost_estimate=pl.CostEstimate(
            flops=2 * groups * tok * width * hid * experts,
            bytes_accessed=2 * experts * width * hid + 12 * groups * tok * width,
            transcendentals=groups * tok * hid * experts,
        ),
    )(place, *grads, *inputs, turned, first, second, pre, back)


def per_device(
    grad_out,
    saved_input,
    expert_ids,
    gate_weights,
    up_weight,
    down_weight,
    engram_gate,
    memory_owner,
    memory_slot,
):
    tok, width = grad_out.shape
    lookups, top = engram_gate.shape[1], expert_ids.shape[1]
    groups = lax.axis_size("expert")
    planes = lax.axis_size("dp") // 4
    part = SHARD // groups
    me = lax.axis_index("dp")
    plane = me // 4
    place = jnp.stack([me, lax.axis_index("expert")]).astype(jnp.int32)
    others = range(1, groups)
    fence = lax.optimization_barrier

    packed, rows = prepare(
        up_weight,
        down_weight,
        grad_out,
        expert_ids,
        gate_weights,
        engram_gate,
        memory_owner,
        memory_slot,
    )
    orders = arrivals(planes)
    came = {}
    zero = (0,) * planes

    def along(step, line):
        even = over_even(line[0]) if step < planes - 1 else None
        return swap(line[1], 4), even

    def arrival(number):
        by_plane = [came[order[number][0]][order[number][1]] for order in orders]
        offsets = tuple(order[number][2] for order in orders)
        return pick(by_plane, plane), offsets

    def plus(share, came_in):
        return (share.astype(jnp.float32) + came_in.astype(jnp.float32)).astype(jnp.bfloat16)

    def reduce(step, sums):
        odd, even = partials[planes - step], partials[step]
        if step > 1 and sums[1] is not None:
            odd = plus(odd, sums[1])
        even = over_even(plus(even, sums[0])) if step > 1 else None
        return swap(odd, 4), even

    half = width // ORDERS
    fits = planes > 3 and folded(lookups // ORDERS * part, half, packed.shape)
    shape = packed.shape if fits else (lookups * part, half)


    rows_x = swap(rows, 2)
    got = [over_expert(rows, step) for step in others]
    came[1] = along(1, (packed, packed))
    late, rows_x = fence((packed, rows_x))
    rows_x, got, near = fence((rows_x, got, swap(rows, 1)))
    grads = [rows] + got
    far = [over_expert(rows_x, step) for step in others]
    near = [near, swap(rows_x, 1)]
    if planes > 2:
        came[2] = along(2, came[1])
        got, far = fence((got, far))
        near, came[2] = fence((near, came[2]))
    blocks = [rows, rows_x, *near, *got, *far]
    for block in got + far:
        blocks += [swap(block[: tok // 2], 1), swap(block[tok // 2 :], 1)]
    partials = table_sums(blocks, place, lookups, part, range(planes), shape)
    for step in range(3, planes - 1 if fits else planes):
        came[step] = along(step, came[step - 1])
    if fits:
        ends = jnp.logical_or(plane == 0, plane == planes - 1)
        met = swap(jnp.where(ends, partials[planes - 1], came[planes - 2][1]), 4)
        came[planes - 1] = (met, None)

    value, where = arrival(0)
    pair = jnp.stack([late, value])
    pair_x = swap(pair, 2)
    later, far = fence((saved_input, far))
    inputs = [over_expert(later, step) for step in others]

    pieces = [(pair, ((zero, 0), (where, 0)))]
    passed, passed_at = pair_x, ((zero, 2), (where, 2))
    todo, near, near_at = pieces[:1], [], []
    sums = ()

    def across(entries):
        return [
            (swap(array, 1), tuple((offsets, flip + 1) for offsets, flip in at))
            for array, at in entries
        ]

    for number in range(2, planes):
        value, where = arrival(number - 1)
        if number == 2:
            partials, value, passed = fence((partials, value, passed))
        else:
            value, passed, inputs = fence((value, passed, inputs))
        pieces += [(passed, passed_at)] + list(zip(near, near_at))
        todo += [(passed, passed_at)]
        moved = across(todo)
        near, near_at = [array for array, _ in moved], [at for _, at in moved]
        passed, passed_at = swap(value, 2), ((where, 2),)
        pieces += [(value, ((where, 0),))]
        todo = [(value, ((where, 0),))]
        if number + 1 == planes:
            moved = across(todo)
            near, near_at = near + [moved[0][0]], near_at + [moved[0][1]]
            todo = []
    pieces += list(zip(near, near_at)) + across(todo)
    inputs = [saved_input] + inputs
    last = (passed_at[0][0], 2)
    hidden = hidden_layers(grads, inputs, pieces, last, place)

    if fits:
        sums = met, None
    for step in range(2 if fits else 1, planes - 1):
        sums = reduce(step, sums)
    sums, hidden, passed = fence((sums, hidden, passed))
    first, second = passed, swap(passed, 1)

    def results(some, begin, dtype):
        return expert_results(
            [grads[g] for g in some],
            [inputs[g] for g in some],
            hidden,
            first,
            second,
            last,
            place,
            lookups,
            top,
            begin * tok,
            dtype,
        )

    if groups > 1:
        rest = results(others, 1, jnp.bfloat16)
        rest, sums = fence((rest, sums))
    if planes > 1:
        sums = reduce(planes - 1, sums)
    returned = [over_expert(rest[(k - 1) * tok : k * tok], groups - k) for k in others]
    total = results([0], 0, jnp.float32)
    for value in returned:
        total = total + value.astype(jnp.float32)
    sums = [partials[0]] + [came_in for came_in in sums[::-1] if came_in is not None]
    table = table_total(sums, lookups * part, half)
    return total.astype(jnp.bfloat16), table.reshape(lookups, part, width // ORDERS)


def solution(mesh):
    return jax.shard_map(
        per_device,
        mesh=mesh,
        in_specs=(
            P(("dp", "expert"), None),
            P(("dp", "expert"), None),
            P(("dp", "expert"), None),
            P(("dp", "expert"), None),
            P("expert", "dp", None),
            P("expert", "dp", None),
            P(("dp", "expert"), None),
            P(("dp", "expert"), None),
            P(("dp", "expert"), None),
        ),
        out_specs=(P(("dp", "expert"), None), P(None, ("dp", "expert"), None)),
        check_vma=False,
    )
```
